32 devices in a mesh: dp: 32 (over z, y, x, core).
Axes of the slice: x: 2, y: 2, z: 4, core: 2. Of those that a mesh axis runs over, the one named last changes fastest.
Arguments:
- tokens: bfloat16 [8192, 2560], P('dp'), may hold values from -6 to 6
- doc_positions: int32 [8192], P('dp'), may hold values from 0 to 255, as said below
- attn_gain: bfloat16 [2560], P('dp'), may hold values from 0.099609375 to 1.8984375
- q_weight: bfloat16 [2560, 2560], P('dp'), may hold values from -0.125 to 0.125
- kv_weight: bfloat16 [2560, 512], P('dp'), may hold values from -0.125 to 0.125
- out_weight: bfloat16 [2560, 2560], P('dp'), may hold values from -0.5 to 0.5
- ffn_gain: bfloat16 [2560], P('dp'), may hold values from 0.099609375 to 1.8984375
- gate_weight: bfloat16 [7680, 2560], P('dp'), may hold values from -0.125 to 0.125
- gate_bias: bfloat16 [7680], P('dp'), may hold values from -3 to 3
- up_weight: bfloat16 [7680, 2560], P('dp'), may hold values from -0.125 to 0.125
- up_bias: bfloat16 [7680], P('dp'), may hold values from -3 to 3
- down_weight: bfloat16 [7680, 2560], P('dp'), may hold values from -0.0625 to 0.0625
- down_bias: bfloat16 [2560], P('dp'), may hold values from -3 to 3
- cotangent: bfloat16 [8192, 2560], P('dp'), may hold values from -6 to 6
Outputs:
- output: bfloat16 [8192, 2560], P('dp')
- input_grad: bfloat16 [8192, 2560], P('dp')
- attn_gain_grad: float32 [2560], P('dp')
- q_grad: float32 [2560, 2560], P('dp')
- kv_grad: float32 [2560, 512], P('dp')
- out_grad: float32 [2560, 2560], P('dp')
- ffn_gain_grad: float32 [2560], P('dp')
- gate_grad: float32 [7680, 2560], P('dp')
- gate_bias_grad: float32 [7680], P('dp')
- up_grad: float32 [7680, 2560], P('dp')
- up_bias_grad: float32 [7680], P('dp')
- down_grad: float32 [7680, 2560], P('dp')
- down_bias_grad: float32 [2560], P('dp')
The draws below stay inside these ranges and needn't reach their ends.
Inputs may be any that keep to these rules, and one draw needn't show every extreme that they name: doc_positions[t] is token t's index within its document; documents lie within one sequence of 256 tokens and a token's position is 0 or one more than the previous token's; in one sequence of every draw a single document fills the whole sequence.
All inputs are finite; a program needn't handle non-finite values.
Results may differ from the reference program's by a relative error of at most 0.014.
Values may be sent and summed in bfloat16 or wider, within the bound.
No kernel may reach another device: no remote copies, remote signals or barrier semaphores. Data moves between devices by JAX's collectives and lax.ppermute only.
A program may use at most 832 MiB of HBM per device.

```python
import math
from functools import partial
import jax
import jax.numpy as jnp
from jax import lax

D = 2560
H = 10
HD = 256
FF = 7680
LENGTH = 256
TOKENS = 8192


def draw_doc_positions(key, part):
    key = jax.random.fold_in(key, 7)
    first_key, last_key, cut_key, pick_key = jax.random.split(key, 4)
    seq_count = TOKENS // LENGTH
    margin = max(LENGTH // 4, 1)
    rows = jnp.arange(seq_count, dtype=jnp.int32)[:, None]
    whole = jax.random.randint(pick_key, (), 0, seq_count)
    begin = jax.random.randint(first_key, (seq_count, 1), 1, margin + 1)
    finish = LENGTH - jax.random.randint(last_key, (seq_count, 1), 1, margin + 1)
    begin = jnp.where(rows == whole, 0, begin)
    finish = jnp.where(rows == whole, LENGTH, finish)
    index = jnp.arange(LENGTH, dtype=jnp.int32)[None, :]
    cuts = jax.random.randint(cut_key, (seq_count, LENGTH), 0, 4) == 0
    outside = (index < begin) | (index > finish)
    boundary = (index == 0) | (index == begin) | (index == finish) | cuts & outside
    starts = lax.cummax(jnp.where(boundary, index, 0), axis=1)
    return (index - starts).reshape(TOKENS).astype(jnp.int32)


def shard_levels(key, extent, pieces, low, high):
    level = 1.0
    for axis_at, parts in pieces:
        steps = jax.random.uniform(jax.random.fold_in(jax.random.fold_in(key, 6), axis_at), (parts,), jnp.float32, low / len(pieces), high / len(pieces))
        level = level * jnp.repeat(jnp.exp(steps), extent[axis_at] // parts).reshape((-1,) + (1,) * (len(extent) - 1 - axis_at))
    return level


def noise(rng, extent, scale, most, shards=(), kind=jnp.bfloat16):
    values = scale * jax.random.normal(rng, extent, jnp.float32)
    if shards:
        values = values * shard_levels(rng, extent, shards, -0.22, 0.18)
    return jnp.clip(values, -most, most).astype(kind)


def setup_inputs(seed: int = 0) -> dict:
    key_list = jax.random.split(jax.random.key(seed), 15)
    tokens = noise(key_list[0], (TOKENS, D), 1.0, 6.0, ((0, 32),))
    doc_positions = draw_doc_positions(jax.random.fold_in(key_list[14], 71), 0)
    attn_gain = jnp.clip(1.0 + 0.18 * jax.random.normal(key_list[2], (D,), jnp.float32), 0.099609375, 1.8984375).astype(jnp.bfloat16)
    q_weight = noise(key_list[3], (D, H * HD), D ** -0.5, 0.125, ((0, 32),))
    kv_weight = noise(key_list[4], (D, 2 * HD), D ** -0.5, 0.125, ((0, 32),))
    out_weight = noise(key_list[5], (H * HD, D), (D // 16) ** -0.5, 0.5, ((0, 32),))
    ffn_gain = jnp.clip(1.0 + 0.18 * jax.random.normal(key_list[6], (D,), jnp.float32), 0.099609375, 1.8984375).astype(jnp.bfloat16)
    gate_weight = noise(key_list[7], (FF, D), D ** -0.5, 0.125, ((0, 32),))
    gate_bias = noise(key_list[8], (FF,), 0.5, 3.0, ((0, 32),))
    up_weight = noise(key_list[9], (FF, D), D ** -0.5, 0.125, ((0, 32),))
    up_bias = noise(key_list[10], (FF,), 0.5, 3.0, ((0, 32),))
    down_weight = noise(key_list[11], (FF, D), FF ** -0.5, 0.0625, ((0, 32),))
    down_bias = noise(key_list[12], (D,), 0.5, 3.0, ((0, 32),))
    cotangent = noise(key_list[13], (TOKENS, D), 1.0, 6.0, ((0, 32),))
    return dict(tokens=tokens, doc_positions=doc_positions, attn_gain=attn_gain, q_weight=q_weight, kv_weight=kv_weight, out_weight=out_weight, ffn_gain=ffn_gain, gate_weight=gate_weight, gate_bias=gate_bias, up_weight=up_weight, up_bias=up_bias, down_weight=down_weight, down_bias=down_bias, cotangent=cotangent)


@jax.custom_vjp
def low(v):
    return lax.optimization_barrier(v.astype(jnp.bfloat16)).astype(jnp.float32)

@jax.custom_vjp
def low_back(v):
    return v

def low_keep(v):
    return (low(v), None)

def low_pass(kept, grad):
    return (grad,)

def back_keep(v):
    return (v, None)

def back_low(kept, grad):
    return (low(grad),)
low.defvjp(low_keep, low_pass)
low_back.defvjp(back_keep, back_low)
epsilon = 1e-06

def rms_scale(values, gain):
    return values * lax.rsqrt(lax.optimization_barrier(jnp.mean(values * values, axis=-1, keepdims=True)) + epsilon) * gain

def angles(positions):
    quarter = HD // 4
    ladder = jnp.arange(quarter, dtype=jnp.float32)
    freq = 10000.0 ** (-2.0 * ladder / (HD // 2))
    angle = positions.astype(jnp.float32)[:, None] * freq[None, :]
    return (jnp.cos(angle), jnp.sin(angle))

def rotate(values, cosine, sine):
    quarter = cosine.shape[-1]
    first = values[..., :quarter]
    second = values[..., quarter:2 * quarter]
    rest = values[..., 2 * quarter:]
    return jnp.concatenate([first * cosine - second * sine, second * cosine + first * sine, rest], -1)

def attend_group(block):
    query, key, value, positions = block
    logit_matrix = jnp.einsum('gqhd,gkd->ghqk', query, key, precision=lax.Precision.HIGHEST)
    logit_matrix = low_back(logit_matrix)
    index = jnp.arange(LENGTH)
    distance = index[:, None] - index[None, :]
    allowed = (distance[None] >= 0) & (distance[None] <= positions[:, :, None])
    logit_matrix = jnp.where(allowed[:, None], logit_matrix, -1e+30)
    top = lax.optimization_barrier(jnp.max(logit_matrix, axis=-1, keepdims=True))
    weights = jnp.exp(logit_matrix - top)
    probs = low(weights / lax.optimization_barrier(jnp.sum(weights, axis=-1, keepdims=True)))
    return jnp.einsum('ghqk,gkd->gqhd', probs, value, precision=lax.Precision.HIGHEST)

def forward(positions, x, gain_one, w_query, w_keyval, w_out, gain_two, w_gate, b_gate, w_up, b_up, w_down, b_down):
    matmul = partial(jnp.dot, precision=lax.Precision.HIGHEST)
    count = x.shape[0]
    seq_count = count // LENGTH
    group = math.gcd(seq_count, max(1, 4096 // LENGTH))
    rounds = seq_count // group
    cosine, sine = angles(positions)
    norm_one = low(rms_scale(x, gain_one))
    q_lin = low_back(matmul(norm_one, w_query)).reshape(count, H, HD)
    kv_lin = low_back(matmul(norm_one, w_keyval))
    query = low(rotate(q_lin, cosine[:, None, :], sine[:, None, :]) * HD ** (-0.5))
    key = low(rotate(kv_lin[:, :HD], cosine, sine))
    value = low(kv_lin[:, HD:])
    blocks = (query.reshape(rounds, group, LENGTH, H, HD), key.reshape(rounds, group, LENGTH, HD), value.reshape(rounds, group, LENGTH, HD), positions.reshape(rounds, group, LENGTH))
    attended = lax.map(jax.checkpoint(attend_group), blocks)
    attended = low(low_back(attended.reshape(count, H * HD)))
    hidden_one = x + low_back(matmul(attended, w_out))
    norm_two = low(rms_scale(hidden_one, gain_two))
    gate = low_back(matmul(norm_two, w_gate.T) + b_gate)
    up = low_back(matmul(norm_two, w_up.T) + b_up)
    act = low(jax.nn.gelu(gate, approximate=True) * up)
    return hidden_one + low_back(matmul(act, w_down) + b_down)

def reference(tokens, doc_positions, attn_gain, q_weight, kv_weight, out_weight, ffn_gain, gate_weight, gate_bias, up_weight, up_bias, down_weight, down_bias, cotangent):
    params = [tokens, attn_gain, q_weight, kv_weight, out_weight, ffn_gain, gate_weight, gate_bias, up_weight, up_bias, down_weight, down_bias]
    params = [p.astype(jnp.float32) for p in params]
    result, pullback = jax.vjp(partial(forward, doc_positions), *params)
    grads = pullback(cotangent.astype(jnp.float32))
    return (result.astype(jnp.bfloat16), grads[0].astype(jnp.bfloat16), grads[1], grads[2], grads[3], grads[4], grads[5], grads[6], grads[7], grads[8], grads[9], grads[10], grads[11])
```

```python
import jax
import jax.numpy as jnp
from jax import lax
from jax.sharding import PartitionSpec as P

D = 2560
H = 10
HD = 256
LENGTH = 256
F32 = jnp.float32
BF = jnp.bfloat16
EPS = 1e-06


def rms_scale(values, gain):
    return values * lax.rsqrt(jnp.mean(values * values, axis=-1, keepdims=True) + EPS) * gain


def angles(positions):
    quarter = HD // 4
    ladder = jnp.arange(quarter, dtype=F32)
    freq = 10000.0 ** (-2.0 * ladder / (HD // 2))
    angle = positions.astype(F32)[:, None] * freq[None, :]
    return (jnp.cos(angle), jnp.sin(angle))


def rotate(values, cosine, sine):
    quarter = cosine.shape[-1]
    first = values[..., :quarter]
    second = values[..., quarter : 2 * quarter]
    rest = values[..., 2 * quarter :]
    return jnp.concatenate(
        [first * cosine - second * sine, second * cosine + first * sine, rest], -1
    )


def dot_tn(left, right, out=F32):
    return lax.dot_general(
        left, right, (((0,), (0,)), ((), ())), preferred_element_type=F32
    ).astype(out)


def dot_nt(left, right):
    return lax.dot_general(left, right, (((1,), (1,)), ((), ())), preferred_element_type=F32)


def dot_nn(left, right):
    return jnp.dot(left, right, preferred_element_type=F32)


def glu_tanh(gate, up):
    return jax.nn.gelu(gate, approximate=True) * up


class Moves:
    def __init__(self, n):
        self.n = n
        self.planes = n // 8
        me = lax.axis_index("dp")
        self.core = me % 2
        self.x = (me // 2) % 2
        self.y = (me // 4) % 2
        self.z = me // 8

    def flip(self, value, bit):
        return lax.ppermute(value, "dp", [(i, i ^ bit) for i in range(self.n)])

    def other(self, value):
        return self.flip(value, 1)

    def over_x(self, value):
        return self.flip(value, 2)

    def over_y(self, value):
        return self.flip(value, 4)

    def up(self, value, steps=1):
        return lax.ppermute(value, "dp", [(i, (i + 8 * steps) % self.n) for i in range(self.n)])


def plane_gather(mv, value):
    half = value.shape[0] // 2
    from_x = mv.over_x(value)
    from_y = mv.over_y(value)
    diag_a = mv.over_y(from_x[:half])
    diag_b = mv.over_x(from_y[half:])
    return value, from_x, from_y, diag_a, diag_b


def plane_scatter(mv, own, to_x, to_y, to_diag):
    half = own.shape[0] // 2
    diag_a = mv.over_x(to_diag[:half].astype(BF))
    diag_b = mv.over_y(to_diag[half:].astype(BF))
    x_a = mv.over_x(to_x[:half].astype(BF))
    y_b = mv.over_y(to_y[half:].astype(BF))
    x_b = mv.over_x((to_x[half:].astype(F32) + diag_b.astype(F32)).astype(BF))
    y_a = mv.over_y((to_y[:half].astype(F32) + diag_a.astype(F32)).astype(BF))
    got_x = jnp.concatenate([x_a, x_b], 0).astype(F32)
    got_y = jnp.concatenate([y_a, y_b], 0).astype(F32)
    return own.astype(F32) + got_x + got_y


def gather_rows(mv, value):
    rows, width = value.shape
    whole = jnp.zeros((mv.n * rows, width), value.dtype)
    half = rows // 2

    def place(whole, block, z, y, x, core, shift=0):
        index = ((z * 2 + y) * 2 + x) * 2 + core
        return lax.dynamic_update_slice(whole, block, (index * rows + shift, 0))

    piece = value
    for step in range(mv.planes):
        z = (mv.z - step) % mv.planes
        own, from_x, from_y, diag_a, diag_b = plane_gather(mv, piece)
        for block, y, x, shift in (
            (own, mv.y, mv.x, 0),
            (from_x, mv.y, 1 - mv.x, 0),
            (from_y, 1 - mv.y, mv.x, 0),
            (diag_a, 1 - mv.y, 1 - mv.x, 0),
            (diag_b, 1 - mv.y, 1 - mv.x, half),
        ):
            whole = place(whole, block, z, y, x, mv.core, shift)
            whole = place(whole, mv.other(block), z, y, x, 1 - mv.core, shift)
        if step < mv.planes - 1:
            piece = mv.up(piece)
    return whole


def gather_tokens(mv, value):
    pieces = []
    piece = value
    for step in range(mv.planes):
        pieces.append(jnp.concatenate([piece, mv.other(piece)], 0))
        if step < mv.planes - 1:
            piece = mv.up(piece)
    return pieces


class RingSum:
    def __init__(self, mv):
        self.mv = mv
        self.got = None
        self.given = 0

    def give(self, piece):
        rows = piece.shape[0] // 2
        total = piece[:rows] + self.mv.other(piece[rows:].astype(BF)).astype(F32)
        return self.add(total)

    def add(self, total):
        if self.got is not None:
            total = total + self.got.astype(F32)
        self.given += 1
        if self.given == self.mv.planes:
            return total
        self.got = self.mv.up(total.astype(BF))
        return None


def scatter_rows(mv, grads):
    width = grads.shape[1]
    rows = grads.shape[0] // mv.n
    blocks = grads.reshape(mv.planes, 2, 2, 2 * rows, width)

    def block(z, y, x):
        return lax.dynamic_slice(blocks, (z, y, x, 0, 0), (1, 1, 1, 2 * rows, width)).reshape(
            2 * rows, width
        )

    ring = RingSum(mv)
    total = None
    for step in range(1, mv.planes + 1):
        z = (mv.z - step) % mv.planes
        total = ring.add(
            plane_scatter(
                mv,
                block(z, mv.y, mv.x),
                block(z, mv.y, 1 - mv.x),
                block(z, 1 - mv.y, mv.x),
                block(z, 1 - mv.y, 1 - mv.x),
            )
        )
    mine = lax.dynamic_slice(total, (mv.core * rows, 0), (rows, width))
    theirs = mv.other(lax.dynamic_slice(total, ((1 - mv.core) * rows, 0), (rows, width)))
    first = jnp.where(mv.core == 0, mine, theirs)
    second = jnp.where(mv.core == 0, theirs, mine)
    return first, second


def scatter_small(mv, vectors):
    count = len(vectors)
    part = vectors[0].shape[0] // mv.n
    value = jnp.stack(vectors).reshape(count, mv.planes, 2, 2, 2, part)
    value = value.transpose(2, 3, 4, 1, 0, 5)

    def pick(value, at):
        return lax.dynamic_index_in_dim(value, at, 0, keepdims=False)

    value = pick(value, mv.y) + mv.over_y(pick(value, 1 - mv.y))
    value = pick(value, mv.x) + mv.over_x(pick(value, 1 - mv.x))
    value = pick(value, mv.core) + mv.other(pick(value, 1 - mv.core))
    total = pick(value, mv.z)
    for step in range(1, mv.planes):
        total = total + mv.up(pick(value, (mv.z + step) % mv.planes), step)
    return [total[i] for i in range(count)]


def core_half(mv, value):
    width = value.shape[1] // 2
    mine = jnp.where(mv.core == 0, value[:, :width], value[:, width:])
    theirs = jnp.where(mv.core == 0, value[:, width:], value[:, :width])
    return jnp.concatenate([mine, mv.other(theirs)], 0)


def make_body(n):
    def body(
        tokens,
        doc_positions,
        attn_gain,
        q_weight,
        kv_weight,
        out_weight,
        ffn_gain,
        gate_weight,
        gate_bias,
        up_weight,
        up_bias,
        down_weight,
        down_bias,
        cotangent,
    ):
        mv = Moves(n)
        head_scale = HD ** (-0.5)
        rows = tokens.shape[0]
        seqs = rows // LENGTH
        small = jnp.stack([attn_gain, ffn_gain, down_bias], 1)
        small = jnp.pad(small, ((0, 0), (0, 125)))
        w_qkv = gather_rows(mv, jnp.concatenate([q_weight, kv_weight, small], 1))
        w_query = w_qkv[:, :D]
        w_keyval = w_qkv[:, D : D + 2 * HD]
        small = w_qkv[:, D + 2 * HD :].T.astype(F32)
        gain_one, gain_two, bias_down = small[0], small[1], small[2]
        w_out = gather_rows(mv, out_weight)
        cot_pieces = gather_tokens(mv, cotangent)
        w_down = jnp.concatenate(plane_gather(mv, down_weight), 0)
        w_gate = jnp.concatenate(plane_gather(mv, gate_weight), 0)
        w_up = jnp.concatenate(plane_gather(mv, up_weight), 0)
        biases = jnp.stack([gate_bias, up_bias])
        bias_x = mv.over_x(biases)
        biases = jnp.concatenate(
            [biases, bias_x, mv.over_y(biases), mv.over_y(bias_x)], 1
        ).astype(F32)

        x_value = tokens.astype(F32)
        norm_one_b = rms_scale(x_value, gain_one).astype(BF)
        cosine, sine = angles(doc_positions)
        q_lin = dot_nn(norm_one_b, w_query).reshape(rows, H, HD)
        kv_lin = dot_nn(norm_one_b, w_keyval)
        query = (
            (rotate(q_lin, cosine[:, None, :], sine[:, None, :]) * head_scale)
            .astype(BF)
            .reshape(seqs, LENGTH, H, HD)
        )
        key = rotate(kv_lin[:, :HD], cosine, sine).astype(BF).reshape(seqs, LENGTH, HD)
        value = kv_lin[:, HD:].astype(BF).reshape(seqs, LENGTH, HD)
        index = jnp.arange(LENGTH)
        distance = index[:, None] - index[None, :]
        allowed = (distance[None] >= 0) & (
            distance[None] <= doc_positions.reshape(seqs, LENGTH)[:, :, None]
        )
        logits = jnp.einsum("sqhd,skd->shqk", query, key, preferred_element_type=F32)
        logits = jnp.where(allowed[:, None], logits, -1e30)
        top = jnp.max(logits, axis=-1, keepdims=True)
        weights = jnp.exp(logits - top)
        soft = weights / jnp.sum(weights, axis=-1, keepdims=True)
        probs = soft.astype(BF)
        attended = (
            jnp.einsum("shqk,skd->sqhd", probs, value, preferred_element_type=F32)
            .reshape(rows, H * HD)
            .astype(BF)
        )
        hidden_one = x_value + dot_nn(attended, w_out)
        norm_two_b = rms_scale(hidden_one, gain_two).astype(BF)

        norm_pieces = gather_tokens(mv, norm_two_b)
        out_ring, grad_ring = RingSum(mv), RingSum(mv)
        order = list(range(1, mv.planes)) + [0]
        acts, grad_gates, grad_ups = [], [], []
        for at in order:
            norm_piece, cot_piece = norm_pieces[at], cot_pieces[at]
            gate = dot_nt(norm_piece, w_gate) + biases[0]
            up = dot_nt(norm_piece, w_up) + biases[1]
            grad_act = dot_nt(cot_piece, w_down)
            act, act_back = jax.vjp(glu_tanh, gate, up)
            grad_gate, grad_up = act_back(grad_act)
            act, grad_gate, grad_up = act.astype(BF), grad_gate.astype(BF), grad_up.astype(BF)
            acts.append(act)
            grad_gates.append(grad_gate)
            grad_ups.append(grad_up)
            grad_norm_two = grad_ring.give(dot_nn(grad_gate, w_gate) + dot_nn(grad_up, w_up))
            branch = out_ring.give(dot_nn(act, w_down))
        output = (hidden_one + branch + bias_down).astype(BF)
        _, norm_two_back = jax.vjp(rms_scale, hidden_one, gain_two)
        grad_rms_two, grad_gain_two = norm_two_back(grad_norm_two)
        grad_hidden = cotangent.astype(F32) + grad_rms_two
        grad_hidden_b = grad_hidden.astype(BF)

        acts = jnp.concatenate(acts, 0)
        grad_gates = jnp.concatenate(grad_gates, 0)
        grad_ups = jnp.concatenate(grad_ups, 0)
        norm_all = jnp.concatenate([norm_pieces[i] for i in order], 0)
        cot_all = jnp.concatenate([cot_pieces[i] for i in order], 0)

        def unit_scatter(grads):
            count = grads.shape[0] // 4
            return plane_scatter(mv, *[grads[i * count : (i + 1) * count] for i in range(4)])

        down_grad = unit_scatter(dot_tn(acts, cot_all, BF))
        gate_grad = unit_scatter(dot_tn(grad_gates, norm_all, BF))
        up_grad = unit_scatter(dot_tn(grad_ups, norm_all, BF))
        bias_sums = jnp.stack(
            [jnp.sum(grad_gates, axis=0, dtype=F32), jnp.sum(grad_ups, axis=0, dtype=F32)]
        )
        units = bias_sums.shape[1] // 4
        moved = mv.over_x(
            jnp.concatenate([bias_sums[:, units : 2 * units], bias_sums[:, 3 * units :]], 1)
        )
        bias_sums = (
            bias_sums[:, :units]
            + moved[:, :units]
            + mv.over_y(bias_sums[:, 2 * units : 3 * units] + moved[:, units:])
        )

        attended_both = jnp.concatenate([attended, mv.other(attended)], 0)
        out_first, out_second = scatter_rows(
            mv, dot_tn(attended_both, core_half(mv, grad_hidden_b), BF)
        )
        out_grad = jnp.concatenate([out_first, out_second], 1)

        grad_attended = dot_nt(grad_hidden_b, w_out).astype(BF).reshape(seqs, LENGTH, H, HD)
        grad_probs = jnp.einsum(
            "sqhd,skd->shqk", grad_attended, value, preferred_element_type=F32
        )
        grad_value = jnp.einsum(
            "shqk,sqhd->skd", probs, grad_attended, preferred_element_type=F32
        ).reshape(rows, HD)
        grad_scores = (
            soft * (grad_probs - jnp.sum(grad_probs * soft, axis=-1, keepdims=True))
        ).astype(BF)
        grad_query = jnp.einsum(
            "shqk,skd->sqhd", grad_scores, key, preferred_element_type=F32
        ).reshape(rows, H, HD)
        grad_key = jnp.einsum(
            "shqk,sqhd->skd", grad_scores, query, preferred_element_type=F32
        ).reshape(rows, HD)
        grad_kv_lin = jnp.concatenate([rotate(grad_key, cosine, -sine), grad_value], 1).astype(BF)
        grad_q_lin = (
            rotate(grad_query * head_scale, cosine[:, None, :], -sine[:, None, :])
            .reshape(rows, H * HD)
            .astype(BF)
        )
        norm_both = jnp.concatenate([norm_one_b, mv.other(norm_one_b)], 0)
        lin_half = jnp.concatenate([core_half(mv, grad_q_lin), core_half(mv, grad_kv_lin)], 1)
        first, second = scatter_rows(mv, dot_tn(norm_both, lin_half, BF))
        q_grad = jnp.concatenate([first[:, : D // 2], second[:, : D // 2]], 1)
        kv_grad = jnp.concatenate([first[:, D // 2 :], second[:, D // 2 :]], 1)

        grad_norm_one = dot_nt(grad_q_lin, w_query) + dot_nt(grad_kv_lin, w_keyval)
        _, norm_one_back = jax.vjp(rms_scale, x_value, gain_one)
        grad_rms_one, grad_gain_one = norm_one_back(grad_norm_one)
        input_grad = (grad_hidden + grad_rms_one).astype(BF)
        down_bias_sum = jnp.sum(cotangent, axis=0, dtype=F32)
        attn_gain_grad, ffn_gain_grad, down_bias_grad = scatter_small(
            mv, [grad_gain_one, grad_gain_two, down_bias_sum]
        )
        return (
            output,
            input_grad,
            attn_gain_grad,
            q_grad,
            kv_grad,
            out_grad,
            ffn_gain_grad,
            gate_grad,
            bias_sums[0],
            up_grad,
            bias_sums[1],
            down_grad,
            down_bias_grad,
        )

    return body


def solution(mesh):
    matrix, vector = P("dp", None), P("dp")
    return jax.shard_map(
        make_body(mesh.shape["dp"]),
        mesh=mesh,
        in_specs=(
            matrix,
            vector,
            vector,
            matrix,
            matrix,
            matrix,
            vector,
            matrix,
            vector,
            matrix,
            vector,
            matrix,
            vector,
            matrix,
        ),
        out_specs=(
            matrix,
            matrix,
            vector,
            matrix,
            matrix,
            matrix,
            vector,
            matrix,
            vector,
            matrix,
            vector,
            matrix,
            vector,
        ),
        check_vma=False,
    )
```

```python
import functools

import jax
import jax.numpy as jnp
from jax import lax
from jax.experimental import pallas as pl
from jax.experimental.pallas import tpu as pltpu
from jax.experimental.layout import Layout, with_layout_constraint
from jax.sharding import PartitionSpec as P

D = 2560
H = 10
HD = 256
LENGTH = 256
F32 = jnp.float32
BF = jnp.bfloat16
EPS = 1e-06


ROWS = Layout((0, 1))


def row_major(value):
    return with_layout_constraint(value, ROWS)


def rms_scale(values, gain):
    return values * lax.rsqrt(jnp.mean(values * values, axis=-1, keepdims=True) + EPS) * gain


def angles(positions):
    quarter = HD // 4
    ladder = jnp.arange(quarter, dtype=F32)
    freq = 10000.0 ** (-2.0 * ladder / (HD // 2))
    angle = positions.astype(F32)[:, None] * freq[None, :]
    return (jnp.cos(angle), jnp.sin(angle))


def rotate(values, cosine, sine):
    quarter = cosine.shape[-1]
    first = values[..., :quarter]
    second = values[..., quarter : 2 * quarter]
    rest = values[..., 2 * quarter :]
    return jnp.concatenate(
        [first * cosine - second * sine, second * cosine + first * sine, rest], -1
    )


def dot_tn(left, right, out=F32):
    return lax.dot_general(
        left, right, (((0,), (0,)), ((), ())), preferred_element_type=F32
    ).astype(out)


def dot_nt(left, right):
    return lax.dot_general(left, right, (((1,), (1,)), ((), ())), preferred_element_type=F32)


def dot_nn(left, right):
    return jnp.dot(left, right, preferred_element_type=F32)


def glu_tanh(gate, up):
    return jax.nn.gelu(gate, approximate=True) * up


class Moves:
    def __init__(self, n):
        self.n = n
        self.planes = n // 8
        me = lax.axis_index("dp")
        self.core = me % 2
        self.x = (me // 2) % 2
        self.y = (me // 4) % 2
        self.z = me // 8

    def flip(self, value, bit):
        return lax.ppermute(value, "dp", [(i, i ^ bit) for i in range(self.n)])

    def other(self, value):
        return self.flip(value, 1)

    def over_x(self, value):
        return self.flip(value, 2)

    def over_y(self, value):
        return self.flip(value, 4)

    def lines(self):
        return [[z * 8 + at + core for z in range(self.planes) for core in (0, 1)] for at in (0, 2, 4, 6)]

    def squares(self):
        return [
            [z * 8 + at + core for at in (0, 2, 4, 6)]
            for z in range(self.planes)
            for core in (0, 1)
        ]

    def up(self, value, steps=1):
        return lax.ppermute(value, "dp", [(i, (i + 8 * steps) % self.n) for i in range(self.n)])


def fence(values):
    return lax.optimization_barrier(values)


def place_kernel(at_ref, mine, theirs, *refs):
    whole = refs[-1]

    @pl.when(pl.program_id(0) < 4)
    def _():
        whole[...] = mine[...]

    @pl.when(pl.program_id(0) >= 4)
    def _():
        whole[...] = theirs[...]


class Rows:
    def __init__(self, mv, rows, width, dtype):
        self.mv, self.rows = mv, rows
        self.shape = jax.ShapeDtypeStruct((mv.n * rows, width), dtype)
        self.whole = None

    def put(self, step, blocks):
        mv, rows = self.mv, self.rows
        z = (mv.z - step) % mv.planes
        at = [
            ((z * 2 + (mv.y ^ fy)) * 2 + (mv.x ^ fx)) * 2 + (mv.core ^ flip)
            for flip in (0, 1)
            for fy in (0, 1)
            for fx in (0, 1)
        ]
        if rows % 16:
            whole = self.whole
            if whole is None:
                whole = jnp.zeros(self.shape.shape, self.shape.dtype)
            for j in range(8):
                block = blocks[j // 4][(j % 4) * rows : (j % 4 + 1) * rows]
                whole = lax.dynamic_update_slice(whole, block, (at[j] * rows, 0))
            self.whole = whole
            return
        width = self.shape.shape[1]
        before = [] if self.whole is None else [self.whole]
        self.whole = pl.pallas_call(
            place_kernel,
            out_shape=self.shape,
            grid_spec=pltpu.PrefetchScalarGridSpec(
                num_scalar_prefetch=1,
                grid=(8,),
                in_specs=[
                    pl.BlockSpec((rows, width), lambda j, at: (jnp.minimum(j, 3), 0)),
                    pl.BlockSpec((rows, width), lambda j, at: (jnp.maximum(j - 4, 0), 0)),
                ]
                + [pl.BlockSpec(memory_space=pl.ANY)] * len(before),
                out_specs=pl.BlockSpec((rows, width), lambda j, at: (at[j], 0)),
            ),
            input_output_aliases={3: 0} if before else {},
            name="place_rows",
        )(jnp.stack(at).astype(jnp.int32), *blocks, *before)

    def done(self):
        return row_major(self.whole)


def gather_weights(mv, to_all, late, late_round, block, block_rounds):
    halves = [block[: block.shape[0] // 2], block[block.shape[0] // 2 :]]
    arrived = []
    rows = to_all[0].shape[0]
    half = rows // 2
    builders = [Rows(mv, rows, v.shape[1], v.dtype) for v in to_all]
    items = [(i, k) for i in range(len(to_all)) for k in range(mv.planes)]
    piece = list(to_all)
    first = second = whole = None
    starts = []
    for at in range(len(items) + 3):
        placed = [b.whole for b in builders]
        state = (piece, first, second, whole, halves, placed)
        if at <= late_round:
            late, state = fence((late, state))
        else:
            state = fence(state)
        piece, first, second, whole, halves, placed = state
        for builder, value in zip(builders, placed):
            builder.whole = value
        send_x, send_y = [], []
        new_first = new_second = new_whole = None
        fresh = at < len(items)
        if fresh:
            i, k = items[at]
            send_x.append(piece[i])
            send_y.append(piece[i])
        joined = fresh and first is not None and first[1].shape[1] == piece[i].shape[1]
        if first is not None:
            own, from_x, from_y = first
            diag_b, diag_a = from_y[half:rows], from_x[:half]
            if joined or not fresh:
                send_x.append(diag_b)
                send_y.append(diag_a)
            else:
                diag_b, diag_a = mv.over_x(diag_b), mv.over_y(diag_a)
        if send_x:
            got_x = mv.over_x(jnp.concatenate(send_x, 0))
            got_y = mv.over_y(jnp.concatenate(send_y, 0))
        if first is not None:
            if joined or not fresh:
                start = rows if fresh else 0
                diag_b, diag_a = got_x, got_y
            else:
                start = 0
            new_second = (own, from_x, from_y, diag_a, diag_b)
            starts.append(start)
        if fresh:
            new_first = (piece[i], got_x, got_y)
            if k < mv.planes - 1:
                piece[i] = mv.up(piece[i])
        if second is not None:
            own, from_x, from_y, diag_a, diag_b = second
            start = starts[at - 2]
            block = jnp.concatenate(
                [
                    own,
                    from_x[:rows],
                    from_y[:rows],
                    diag_a[start : start + half],
                    diag_b[start : start + half],
                ],
                0,
            )
            new_whole = (block, mv.other(block))
        if at in block_rounds:
            which = block_rounds.index(at) % 2
            halves[which] = mv.up(halves[which])
            arrived.append(halves[which])
        if whole is not None:
            i, k = items[at - 3]
            builders[i].put(k, whole)
        first, second, whole = new_first, new_second, new_whole
    arrived = [jnp.concatenate(arrived[i : i + 2], 0) for i in range(0, len(arrived), 2)]
    return [b.done() for b in builders], late, arrived


def mine_of(mv, value, axis=0):
    size = value.shape[axis] // 2
    return lax.dynamic_slice_in_dim(value, mv.core * size, size, axis)


def theirs_of(mv, value, axis=0):
    size = value.shape[axis] // 2
    return lax.dynamic_slice_in_dim(value, (1 - mv.core) * size, size, axis)


def scatter_grads(mv, arrays, arrays_rows, held, work):
    rows = arrays_rows // (mv.n // 2)
    half = rows // 2

    def block(array, step, flip_y, flip_x, shift=0, count=rows):
        index = (((mv.z - step) % mv.planes) * 2 + (mv.y ^ flip_y)) * 2 + (mv.x ^ flip_x)
        return lax.dynamic_slice(array, (index * rows + shift, 0), (count, array.shape[1]))

    items = [(i, k) for i in range(len(arrays)) for k in [*range(1, mv.planes), 0]]
    rings = [None] * len(arrays)
    sources = [None] * len(arrays)
    results = {}
    starts = []
    first = second = None
    for at in range(max(len(items) + 2, mv.planes + 6)):
        if at < len(items) and sources[items[at][0]] is None:
            sources[items[at][0]] = arrays[items[at][0]]()
        first, second, sources, rings, results, now = fence(
            (first, second, sources, rings, results, held)
        )
        held.update(now)
        new_first = new_second = None
        send_x, send_y = [], []
        fresh = at < len(items)
        if fresh:
            i, k = items[at]
            source = sources[i]
            send_x += [block(source, k, 1, 1, 0, half), block(source, k, 0, 1, 0, half)]
            send_y += [block(source, k, 1, 1, half, half), block(source, k, 1, 0, half, half)]
        if first is not None:
            i, k = items[at - 1]
            from_x, from_y = first
            last_x = block(sources[i], k, 0, 1, half, half).astype(F32) + from_y[:half].astype(F32)
            last_y = block(sources[i], k, 1, 0, 0, half).astype(F32) + from_x[:half].astype(F32)
            last_x, last_y = last_x.astype(BF), last_y.astype(BF)
            joined = fresh and source.shape[1] == last_x.shape[1]
            if joined or not fresh:
                send_x.append(last_x)
                send_y.append(last_y)
                start = 2 * half if fresh else 0
            else:
                more_x, more_y = mv.over_x(last_x), mv.over_y(last_y)
                start = 0
            starts.append(start)
        if send_x:
            got_x = mv.over_x(jnp.concatenate(send_x, 0))
            got_y = mv.over_y(jnp.concatenate(send_y, 0))
        if first is not None:
            if joined or not fresh:
                more_x, more_y = got_x, got_y
            new_second = (from_x, from_y, more_x, more_y)
        if fresh:
            new_first = (got_x, got_y)
        if second is not None:
            i, k = items[at - 2]
            from_x, from_y, more_x, more_y = second
            start = starts[at - 2]
            total = block(sources[i], k, 0, 0).astype(F32)
            total += jnp.concatenate(
                [from_x[half : 2 * half], more_x[start : start + half]], 0
            ).astype(F32)
            total += jnp.concatenate(
                [more_y[start : start + half], from_y[half : 2 * half]], 0
            ).astype(F32)
            if rings[i] is not None:
                total = total + rings[i].astype(F32)
            if k != 0:
                rings[i] = mv.up(total.astype(BF))
            else:
                results[i] = total
        work(at)
        first, second = new_first, new_second
    return [results[i] for i in range(len(arrays))]


def swap_halves(mv, total):
    rows = total.shape[0] // 2
    mine = lax.dynamic_slice(total, (mv.core * rows, 0), (rows, total.shape[1]))
    theirs = mv.other(lax.dynamic_slice(total, ((1 - mv.core) * rows, 0), (rows, total.shape[1])))
    return jnp.where(mv.core == 0, mine, theirs), jnp.where(mv.core == 0, theirs, mine)


def core_half(mv, value):
    width = value.shape[1] // 2
    mine = jnp.where(mv.core == 0, value[:, :width], value[:, width:])
    theirs = jnp.where(mv.core == 0, value[:, width:], value[:, :width])
    return jnp.concatenate([mine, mv.other(theirs)], 0)


def make_body(n):
    def body(
        tokens,
        doc_positions,
        attn_gain,
        q_weight,
        kv_weight,
        out_weight,
        ffn_gain,
        gate_weight,
        gate_bias,
        up_weight,
        up_bias,
        down_weight,
        down_bias,
        cotangent,
    ):
        mv = Moves(n)
        head_scale = HD ** (-0.5)
        rows = tokens.shape[0]
        seqs = rows // LENGTH
        small = jnp.stack([attn_gain, ffn_gain, down_bias], 1)
        small = jnp.pad(small, ((0, 0), (0, 125)))
        units = gate_weight.shape[0]
        padded = -(-(units + 2) // 128) * 128

        def pad_rows(value):
            return jnp.pad(value, ((0, padded - units), (0, 0)))

        bias_rows = jnp.pad(
            jnp.stack([gate_bias, up_bias]), ((0, padded - units - 2), (0, D - units))
        )
        ffn = jnp.concatenate(
            [pad_rows(down_weight), gate_weight, bias_rows, pad_rows(up_weight)], 0
        )
        rounds = 2 * mv.planes
        (w_qkv, w_out), ffn, cots = gather_weights(
            mv,
            [jnp.concatenate([q_weight, kv_weight, small], 1), out_weight],
            ffn,
            rounds,
            cotangent,
            list(range(rounds - 3, rounds + 3)),
        )
        cots = [cotangent, *cots]
        ffn = lax.all_gather(ffn, "dp", axis=0, tiled=True, axis_index_groups=mv.squares())
        w_query = w_qkv[:, :D]
        w_keyval = w_qkv[:, D : D + 2 * HD]
        small = w_qkv[:, D + 2 * HD :].T.astype(F32)
        gain_one, gain_two, bias_down = small[0], small[1], small[2]

        x_value = tokens.astype(F32)
        norm_one_b = rms_scale(x_value, gain_one).astype(BF)
        cosine, sine = angles(doc_positions)
        q_lin = dot_nn(norm_one_b, w_query).reshape(rows, H, HD)
        kv_lin = dot_nn(norm_one_b, w_keyval)
        query = (
            (rotate(q_lin, cosine[:, None, :], sine[:, None, :]) * head_scale)
            .astype(BF)
            .reshape(seqs, LENGTH, H, HD)
        )
        key = rotate(kv_lin[:, :HD], cosine, sine).astype(BF).reshape(seqs, LENGTH, HD)
        value = kv_lin[:, HD:].astype(BF).reshape(seqs, LENGTH, HD)
        index = jnp.arange(LENGTH)
        distance = index[:, None] - index[None, :]
        allowed = (distance[None] >= 0) & (
            distance[None] <= doc_positions.reshape(seqs, LENGTH)[:, :, None]
        )
        logits = jnp.einsum("sqhd,skd->shqk", query, key, preferred_element_type=F32)
        logits = jnp.where(allowed[:, None], logits, -1e30)
        top = jnp.max(logits, axis=-1, keepdims=True)
        weights = jnp.exp(logits - top)
        soft = weights / jnp.sum(weights, axis=-1, keepdims=True)
        probs = soft.astype(BF)
        attended = (
            jnp.einsum("shqk,skd->sqhd", probs, value, preferred_element_type=F32)
            .reshape(rows, H * HD)
            .astype(BF)
        )
        hidden_one = x_value + dot_nn(attended, w_out)
        norm_two_b = rms_scale(hidden_one, gain_two).astype(BF)

        order = [*range(1, mv.planes), 0]
        norms, cots, norm_pieces, cot_pieces = [norm_two_b], list(cots), [], []
        swap_early = [attended, norm_one_b]
        swapped = []

        def linear(step):
            return dot_nt(norm_pieces[step], w_both) + bias_both, dot_nt(cot_pieces[step], w_down)

        def pick(both, which):
            return jnp.concatenate(
                [
                    both[:, (2 * i + which) * padded : (2 * i + which + 1) * padded]
                    for i in range(4)
                ],
                1,
            )

        def nonlinear(both, grad_act):
            act, act_back = jax.vjp(glu_tanh, pick(both, 0), pick(both, 1))
            grad_gate, grad_up = act_back(grad_act)
            parts = []
            for i in range(4):
                parts.append(grad_gate[:, i * padded : (i + 1) * padded])
                parts.append(grad_up[:, i * padded : (i + 1) * padded])
            grads = jnp.concatenate(parts, 1).astype(BF)
            partial = dot_nn(grads, w_both)
            return act.astype(BF), grads, partial[:rows], partial[rows:].astype(BF)

        acts, grads_all = [], []
        sends, received, parts, gots = {}, None, {}, {}
        last = mv.planes + 1
        for at in range(last + 1):
            norms, cots, swap_early, sends, norm_pieces, cot_pieces, acts, grads_all = fence(
                (norms, cots, swap_early, sends, norm_pieces, cot_pieces, acts, grads_all)
            )
            if at == 1:
                ffn = ffn.reshape(4, 3 * padded, D)
                w_down = ffn[:, :padded].reshape(4 * padded, D)
                w_both = ffn[:, padded:].reshape(8 * padded, D)
                bias_both = ffn[:, padded + units : padded + units + 2, :padded].reshape(8 * padded)
                bias_both = bias_both.astype(F32)
                w_down, w_both, bias_both, norms = fence((w_down, w_both, bias_both, norms))
            if at <= mv.planes - 2:
                norms.append(mv.up(norms[at]))
            if 4 + at < mv.planes:
                cots.append(mv.up(cots[3 + at]))
            if at - 2 in sends:
                received = mv.up(sends.pop(at - 2))
            if at < mv.planes:
                norm_pieces.append(jnp.concatenate([norms[at], mv.other(norms[at])], 0))
                cot_pieces.append(jnp.concatenate([cots[at], mv.other(cots[at])], 0))
            if 1 <= at <= len(swap_early):
                early = swap_early[at - 1]
                swapped.append(jnp.concatenate([early, mv.other(early)], 0))
            step = at - 1
            if 0 <= step < mv.planes:
                act, grads, own_part, their_part = nonlinear(*linear(step))
                acts.append(act)
                grads_all.append(grads)
                parts[step] = own_part
                gots[step] = mv.other(their_part)
            if at == last:
                acts = jnp.concatenate(acts, 0)
                grads_all = jnp.concatenate(grads_all, 0)
                cot_all = jnp.concatenate(cot_pieces, 0)
                norm_all = jnp.concatenate(norm_pieces, 0)
                down_partial = dot_tn(acts, cot_all, BF)
                both_partial = dot_tn(grads_all, norm_all, BF)
                down_partial, both_partial = fence((down_partial, both_partial))
            norms, cots, norm_pieces, cot_pieces, swapped, acts, grads_all, parts, gots, received = (
                fence(
                    (
                        norms,
                        cots,
                        norm_pieces,
                        cot_pieces,
                        swapped,
                        acts,
                        grads_all,
                        parts,
                        gots,
                        received,
                    )
                )
            )
            if step >= 1:
                done = step if step < mv.planes else 0
                total = parts.pop(done) + gots.pop(done).astype(F32)
                if received is not None:
                    total = total + received.astype(F32)
                    received = None
                if done:
                    sends[done] = total.astype(BF)
        grad_norm_two = total
        attended_both, norm_both = swapped
        ffn_groups = mv.squares()
        down_sum = lax.psum_scatter(
            down_partial, "dp", scatter_dimension=0, tiled=True, axis_index_groups=ffn_groups
        )
        both_sum = lax.psum_scatter(
            both_partial, "dp", scatter_dimension=0, tiled=True, axis_index_groups=ffn_groups
        )
        _, norm_two_back = jax.vjp(rms_scale, hidden_one, gain_two)
        grad_rms_two, grad_gain_two = norm_two_back(grad_norm_two)
        grad_hidden = cotangent.astype(F32) + grad_rms_two
        grad_hidden_b = grad_hidden.astype(BF)

        half_columns = core_half(mv, grad_hidden_b)
        grad_attended = dot_nt(grad_hidden_b, w_out).astype(BF).reshape(seqs, LENGTH, H, HD)
        out_partial = dot_tn(attended_both, half_columns, BF)
        out_partial, grad_attended, grads_all, acts = fence(
            (out_partial, grad_attended, grads_all, acts)
        )
        held = {"grads": grads_all, "acts": acts, "attended": grad_attended}

        def scores_back(grad_attended):
            grad_probs = jnp.einsum(
                "sqhd,skd->shqk", grad_attended, value, preferred_element_type=F32
            )
            return (
                soft * (grad_probs - jnp.sum(grad_probs * soft, axis=-1, keepdims=True))
            ).astype(BF)

        def lin_back(grad_scores, grad_attended):
            grad_value = jnp.einsum(
                "shqk,sqhd->skd", probs, grad_attended, preferred_element_type=F32
            ).reshape(rows, HD)
            grad_query = jnp.einsum(
                "shqk,skd->sqhd", grad_scores, key, preferred_element_type=F32
            ).reshape(rows, H, HD)
            grad_key = jnp.einsum(
                "shqk,sqhd->skd", grad_scores, query, preferred_element_type=F32
            ).reshape(rows, HD)
            grad_kv_lin = jnp.concatenate(
                [rotate(grad_key, cosine, -sine), grad_value], 1
            ).astype(BF)
            grad_q_lin = (
                rotate(grad_query * head_scale, cosine[:, None, :], -sine[:, None, :])
                .reshape(rows, H * HD)
                .astype(BF)
            )
            return grad_q_lin, grad_kv_lin

        def work(at):
            if at == 0:
                branch = dot_nn(held.pop("acts"), w_down).reshape(mv.planes, 2, rows, D)
                held["own"] = branch[:, 0]
                held["got"] = mv.other(branch[:, 1].astype(BF))
                bias = jnp.sum(held.pop("grads"), axis=0, dtype=F32)
                held["bias"] = bias.reshape(2, 2, 2, padded)[..., :units]
            if at == 1:
                held["scores"] = scores_back(held["attended"])
            if at == 2:
                held["q"], held["kv"] = lin_back(held.pop("scores"), held.pop("attended"))
            if at == 3:
                half = jnp.concatenate([core_half(mv, held["q"]), core_half(mv, held["kv"])], 1)
                held["partial"] = dot_tn(norm_both, half, BF)
                grad_norm_one = dot_nt(held.pop("q"), w_query) + dot_nt(held.pop("kv"), w_keyval)
                _, norm_one_back = jax.vjp(rms_scale, x_value, gain_one)
                grad_rms_one, grad_gain_one = norm_one_back(grad_norm_one)
                held["input_grad"] = (grad_hidden + grad_rms_one).astype(BF)
                down_bias_sum = jnp.sum(cotangent, axis=0, dtype=F32)
                part = D // mv.n
                small = jnp.stack([grad_gain_one, grad_gain_two, down_bias_sum])
                small = small.reshape(3, mv.planes, 2, 2, 2, part).transpose(2, 3, 4, 1, 0, 5)
                held["small"] = small
            for stage, (coordinate, move) in enumerate(
                ((mv.y, mv.over_y), (mv.x, mv.over_x), (mv.core, mv.other))
            ):
                if at == 4 + stage:
                    for name in ("small", "bias")[: 2 if stage < 2 else 1]:
                        whole = held[name]
                        keep = lax.dynamic_index_in_dim(whole, coordinate, 0, keepdims=False)
                        away = lax.dynamic_index_in_dim(whole, 1 - coordinate, 0, keepdims=False)
                        held[name] = keep + move(away)
            step = at - 6
            if 0 < step < mv.planes:
                away = lax.dynamic_index_in_dim(
                    held["small"], (mv.z + step) % mv.planes, 0, keepdims=False
                )
                held["small_sum"] = held.get("small_sum", 0.0) + mv.up(away, step)
            ring = at - 1
            if 0 <= ring < mv.planes:
                at_piece = order[ring]
                branch = held["own"][at_piece] + held["got"][at_piece].astype(F32)
                if ring > 0:
                    branch = branch + held.pop("branch").astype(F32)
                if ring < mv.planes - 1:
                    held["branch"] = mv.up(branch.astype(BF))
                else:
                    held["output"] = (hidden_one + branch + bias_down).astype(BF)

        out_total, lin_total = scatter_grads(
            mv, [lambda: out_partial, lambda: held.pop("partial")], D, held, work
        )
        out_total, lin_total, down_sum, both_sum = fence((out_total, lin_total, down_sum, both_sum))
        small = held["small_sum"] + lax.dynamic_index_in_dim(
            held["small"], mv.z, 0, keepdims=False
        )
        down_grad = down_sum[:units].astype(F32)
        gate_grad = both_sum[:units].astype(F32)
        up_grad = both_sum[padded : padded + units].astype(F32)
        out_grad = jnp.concatenate(swap_halves(mv, out_total), 1)
        first, second = swap_halves(mv, lin_total)
        q_grad = jnp.concatenate([first[:, : D // 2], second[:, : D // 2]], 1)
        kv_grad = jnp.concatenate([first[:, D // 2 :], second[:, D // 2 :]], 1)

        return (
            held["output"],
            held["input_grad"],
            small[0],
            q_grad,
            kv_grad,
            out_grad,
            small[1],
            gate_grad,
            held["bias"][0],
            up_grad,
            held["bias"][1],
            down_grad,
            small[2],
        )

    return body


def solution(mesh):
    matrix, vector = P("dp", None), P("dp")
    return jax.shard_map(
        make_body(mesh.shape["dp"]),
        mesh=mesh,
        in_specs=(
            matrix,
            vector,
            vector,
            matrix,
            matrix,
            matrix,
            vector,
            matrix,
            vector,
            matrix,
            vector,
            matrix,
            vector,
            matrix,
        ),
        out_specs=(
            matrix,
            matrix,
            vector,
            matrix,
            matrix,
            matrix,
            vector,
            matrix,
            vector,
            matrix,
            vector,
            matrix,
            vector,
        ),
        check_vma=False,
    )
```

```python
import functools

import jax
import jax.numpy as jnp
from jax import lax
from jax.experimental import pallas as pl
from jax.experimental.pallas import tpu as pltpu
from jax.experimental.layout import Layout, with_layout_constraint
from jax.sharding import PartitionSpec as P

D = 2560
H = 10
HD = 256
LENGTH = 256
F32 = jnp.float32
BF = jnp.bfloat16
EPS = 1e-06


ROWS = Layout((0, 1))


def row_major(value):
    return with_layout_constraint(value, ROWS)


def rms_scale(values, gain):
    return values * lax.rsqrt(jnp.mean(values * values, axis=-1, keepdims=True) + EPS) * gain


def angles(positions):
    quarter = HD // 4
    ladder = jnp.arange(quarter, dtype=F32)
    freq = 10000.0 ** (-2.0 * ladder / (HD // 2))
    angle = positions.astype(F32)[:, None] * freq[None, :]
    return (jnp.cos(angle), jnp.sin(angle))


def rotate(values, cosine, sine):
    quarter = cosine.shape[-1]
    first = values[..., :quarter]
    second = values[..., quarter : 2 * quarter]
    rest = values[..., 2 * quarter :]
    return jnp.concatenate(
        [first * cosine - second * sine, second * cosine + first * sine, rest], -1
    )


def dot_tn(left, right, out=F32):
    return lax.dot_general(
        left, right, (((0,), (0,)), ((), ())), preferred_element_type=F32
    ).astype(out)


def dot_nt(left, right):
    return lax.dot_general(left, right, (((1,), (1,)), ((), ())), preferred_element_type=F32)


def dot_nn(left, right):
    return jnp.dot(left, right, preferred_element_type=F32)


def glu_tanh(gate, up):
    return jax.nn.gelu(gate, approximate=True) * up


class Moves:
    def __init__(self, n):
        self.n = n
        self.planes = n // 8
        me = lax.axis_index("dp")
        self.core = me % 2
        self.x = (me // 2) % 2
        self.y = (me // 4) % 2
        self.z = me // 8

    def flip(self, value, bit):
        return lax.ppermute(value, "dp", [(i, i ^ bit) for i in range(self.n)])

    def other(self, value):
        return self.flip(value, 1)

    def over_x(self, value):
        return self.flip(value, 2)

    def over_y(self, value):
        return self.flip(value, 4)

    def lines(self):
        return [[z * 8 + at + core for z in range(self.planes) for core in (0, 1)] for at in (0, 2, 4, 6)]

    def squares(self):
        return [
            [z * 8 + at + core for at in (0, 2, 4, 6)]
            for z in range(self.planes)
            for core in (0, 1)
        ]

    def up(self, value, steps=1):
        return lax.ppermute(value, "dp", [(i, (i + 8 * steps) % self.n) for i in range(self.n)])


def fence(values):
    return lax.optimization_barrier(values)


def place_kernel(at_ref, mine, theirs, *refs):
    whole = refs[-1]

    @pl.when(pl.program_id(0) < 4)
    def _():
        whole[...] = mine[...]

    @pl.when(pl.program_id(0) >= 4)
    def _():
        whole[...] = theirs[...]


class Rows:
    def __init__(self, mv, rows, width, dtype):
        self.mv, self.rows = mv, rows
        self.shape = jax.ShapeDtypeStruct((mv.n * rows, width), dtype)
        self.whole = None

    def put(self, step, blocks):
        mv, rows = self.mv, self.rows
        z = (mv.z - step) % mv.planes
        at = [
            ((z * 2 + (mv.y ^ fy)) * 2 + (mv.x ^ fx)) * 2 + (mv.core ^ flip)
            for flip in (0, 1)
            for fy in (0, 1)
            for fx in (0, 1)
        ]
        if rows % 16:
            whole = self.whole
            if whole is None:
                whole = jnp.zeros(self.shape.shape, self.shape.dtype)
            for j in range(8):
                block = blocks[j // 4][(j % 4) * rows : (j % 4 + 1) * rows]
                whole = lax.dynamic_update_slice(whole, block, (at[j] * rows, 0))
            self.whole = whole
            return
        width = self.shape.shape[1]
        before = [] if self.whole is None else [self.whole]
        self.whole = pl.pallas_call(
            place_kernel,
            out_shape=self.shape,
            grid_spec=pltpu.PrefetchScalarGridSpec(
                num_scalar_prefetch=1,
                grid=(8,),
                in_specs=[
                    pl.BlockSpec((rows, width), lambda j, at: (jnp.minimum(j, 3), 0)),
                    pl.BlockSpec((rows, width), lambda j, at: (jnp.maximum(j - 4, 0), 0)),
                ]
                + [pl.BlockSpec(memory_space=pl.ANY)] * len(before),
                out_specs=pl.BlockSpec((rows, width), lambda j, at: (at[j], 0)),
            ),
            input_output_aliases={3: 0} if before else {},
            name="place_rows",
        )(jnp.stack(at).astype(jnp.int32), *blocks, *before)

    def done(self):
        return row_major(self.whole)


def gather_weights(mv, to_all, late, late_round, block, block_rounds, held, work):
    halves = [block[: block.shape[0] // 2], block[block.shape[0] // 2 :]]
    arrived = []
    rows = to_all[0].shape[0]
    half = rows // 2
    builders = [Rows(mv, rows, v.shape[1], v.dtype) for v in to_all]
    items = [(i, k) for i in range(len(to_all)) for k in range(mv.planes)]
    piece = list(to_all)
    first = second = whole = None
    starts = []
    for at in range(len(items) + 3):
        placed = [b.whole for b in builders]
        state = (piece, first, second, whole, halves, placed, held)
        if at <= late_round:
            late, state = fence((late, state))
        else:
            state = fence(state)
        piece, first, second, whole, halves, placed, now = state
        held.update(now)
        for builder, value in zip(builders, placed):
            builder.whole = value
        send_x, send_y = [], []
        new_first = new_second = new_whole = None
        fresh = at < len(items)
        if fresh:
            i, k = items[at]
            send_x.append(piece[i])
            send_y.append(piece[i])
        joined = fresh and first is not None and first[1].shape[1] == piece[i].shape[1]
        if first is not None:
            own, from_x, from_y = first
            diag_b, diag_a = from_y[half:rows], from_x[:half]
            if joined or not fresh:
                send_x.append(diag_b)
                send_y.append(diag_a)
            else:
                diag_b, diag_a = mv.over_x(diag_b), mv.over_y(diag_a)
        if send_x:
            got_x = mv.over_x(jnp.concatenate(send_x, 0))
            got_y = mv.over_y(jnp.concatenate(send_y, 0))
        if first is not None:
            if joined or not fresh:
                start = rows if fresh else 0
                diag_b, diag_a = got_x, got_y
            else:
                start = 0
            new_second = (own, from_x, from_y, diag_a, diag_b)
            starts.append(start)
        if fresh:
            new_first = (piece[i], got_x, got_y)
            if k < mv.planes - 1:
                piece[i] = mv.up(piece[i])
        if second is not None:
            own, from_x, from_y, diag_a, diag_b = second
            start = starts[at - 2]
            block = jnp.concatenate(
                [
                    own,
                    from_x[:rows],
                    from_y[:rows],
                    diag_a[start : start + half],
                    diag_b[start : start + half],
                ],
                0,
            )
            new_whole = (block, mv.other(block))
        if at in block_rounds:
            which = block_rounds.index(at) % 2
            halves[which] = mv.up(halves[which])
            arrived.append(halves[which])
        if whole is not None:
            i, k = items[at - 3]
            builders[i].put(k, whole)
        work(at - mv.planes - 3, placed[0])
        first, second, whole = new_first, new_second, new_whole
    arrived = [jnp.concatenate(arrived[i : i + 2], 0) for i in range(0, len(arrived), 2)]
    return [b.done() for b in builders], late, arrived


def mine_of(mv, value, axis=0):
    size = value.shape[axis] // 2
    return lax.dynamic_slice_in_dim(value, mv.core * size, size, axis)


def theirs_of(mv, value, axis=0):
    size = value.shape[axis] // 2
    return lax.dynamic_slice_in_dim(value, (1 - mv.core) * size, size, axis)


def scatter_grads(mv, arrays, arrays_rows, held, work):
    rows = arrays_rows // (mv.n // 2)
    half = rows // 2

    def block(array, step, flip_y, flip_x, shift=0, count=rows):
        index = (((mv.z - step) % mv.planes) * 2 + (mv.y ^ flip_y)) * 2 + (mv.x ^ flip_x)
        return lax.dynamic_slice(array, (index * rows + shift, 0), (count, array.shape[1]))

    items = [(i, k) for i in range(len(arrays)) for k in [*range(1, mv.planes), 0]]
    rings = [None] * len(arrays)
    sources = [None] * len(arrays)
    starts = []
    first = second = None
    for at in range(max(len(items) + 2, 9 + mv.planes // 2)):
        if at < len(items) and sources[items[at][0]] is None:
            sources[items[at][0]] = arrays[items[at][0]]()
        first, second, sources, rings, now = fence((first, second, sources, rings, held))
        held.update(now)
        new_first = new_second = None
        send_x, send_y = [], []
        fresh = at < len(items)
        if fresh:
            i, k = items[at]
            source = sources[i]
            send_x += [block(source, k, 1, 1, 0, half), block(source, k, 0, 1, 0, half)]
            send_y += [block(source, k, 1, 1, half, half), block(source, k, 1, 0, half, half)]
        if first is not None:
            i, k = items[at - 1]
            from_x, from_y = first
            last_x = block(sources[i], k, 0, 1, half, half).astype(F32) + from_y[:half].astype(F32)
            last_y = block(sources[i], k, 1, 0, 0, half).astype(F32) + from_x[:half].astype(F32)
            last_x, last_y = last_x.astype(BF), last_y.astype(BF)
            joined = fresh and source.shape[1] == last_x.shape[1]
            if joined or not fresh:
                send_x.append(last_x)
                send_y.append(last_y)
                start = 2 * half if fresh else 0
            else:
                more_x, more_y = mv.over_x(last_x), mv.over_y(last_y)
                start = 0
            starts.append(start)
        if send_x:
            send_x, send_y, second, now = fence(
                (jnp.concatenate(send_x, 0), jnp.concatenate(send_y, 0), second, held)
            )
            held.update(now)
            got_x, got_y = mv.over_x(send_x), mv.over_y(send_y)
        if first is not None:
            if joined or not fresh:
                more_x, more_y = got_x, got_y
            new_second = (from_x, from_y, more_x, more_y)
        if fresh:
            new_first = (got_x, got_y)
        if second is not None:
            i, k = items[at - 2]
            from_x, from_y, more_x, more_y = second
            start = starts[at - 2]
            total = block(sources[i], k, 0, 0).astype(F32)
            total += jnp.concatenate(
                [from_x[half : 2 * half], more_x[start : start + half]], 0
            ).astype(F32)
            total += jnp.concatenate(
                [more_y[start : start + half], from_y[half : 2 * half]], 0
            ).astype(F32)
            if rings[i] is not None:
                total = total + rings[i].astype(F32)
            if k != 0:
                rings[i] = mv.up(total.astype(BF))
            else:
                held[f"sum{i}"] = total
        work(at)
        first, second = new_first, new_second


def swap_halves(mv, total):
    rows = total.shape[0] // 2
    mine = lax.dynamic_slice(total, (mv.core * rows, 0), (rows, total.shape[1]))
    theirs = mv.other(lax.dynamic_slice(total, ((1 - mv.core) * rows, 0), (rows, total.shape[1])))
    return jnp.where(mv.core == 0, mine, theirs), jnp.where(mv.core == 0, theirs, mine)


def core_half(mv, value):
    width = value.shape[1] // 2
    mine = jnp.where(mv.core == 0, value[:, :width], value[:, width:])
    theirs = jnp.where(mv.core == 0, value[:, width:], value[:, :width])
    return jnp.concatenate([mine, mv.other(theirs)], 0)


def make_body(n):
    def body(
        tokens,
        doc_positions,
        attn_gain,
        q_weight,
        kv_weight,
        out_weight,
        ffn_gain,
        gate_weight,
        gate_bias,
        up_weight,
        up_bias,
        down_weight,
        down_bias,
        cotangent,
    ):
        mv = Moves(n)
        head_scale = HD ** (-0.5)
        rows = tokens.shape[0]
        seqs = rows // LENGTH
        small = jnp.stack([attn_gain, ffn_gain, down_bias], 1)
        small = jnp.pad(small, ((0, 0), (0, 125)))
        units = gate_weight.shape[0]
        padded = -(-(units + 2) // 128) * 128

        def pad_rows(value):
            return jnp.pad(value, ((0, padded - units), (0, 0)))

        bias_rows = jnp.pad(
            jnp.stack([gate_bias, up_bias]), ((0, padded - units - 2), (0, D - units))
        )
        ffn = jnp.concatenate(
            [pad_rows(down_weight), gate_weight, bias_rows, pad_rows(up_weight)], 0
        )
        rounds = 2 * mv.planes
        x_value = tokens.astype(F32)
        cosine, sine = angles(doc_positions)
        index = jnp.arange(LENGTH)
        distance = index[:, None] - index[None, :]
        allowed = (distance[None] >= 0) & (
            distance[None] <= doc_positions.reshape(seqs, LENGTH)[:, :, None]
        )
        held = {}

        def split_qkv(w_qkv):
            small = w_qkv[:, D + 2 * HD :].T.astype(F32)
            return w_qkv[:, :D], w_qkv[:, D : D + 2 * HD], small

        def attention(at, w_qkv):
            if at == 1:
                w_query, w_keyval, small = split_qkv(w_qkv)
                norm_one_b = rms_scale(x_value, small[0]).astype(BF)
                held["norm_one"] = norm_one_b
                q_lin = dot_nn(norm_one_b, w_query).reshape(rows, H, HD)
                query = rotate(q_lin, cosine[:, None, :], sine[:, None, :]) * head_scale
                held["query"] = query.astype(BF).reshape(seqs, LENGTH, H, HD)
                held["kv"] = dot_nn(norm_one_b, w_keyval)
            if at == 2:
                kv_lin = held.pop("kv")
                key = rotate(kv_lin[:, :HD], cosine, sine).astype(BF)
                held["key"] = key.reshape(seqs, LENGTH, HD)
                held["value"] = kv_lin[:, HD:].astype(BF).reshape(seqs, LENGTH, HD)
                logits = jnp.einsum(
                    "sqhd,skd->shqk", held["query"], held["key"], preferred_element_type=F32
                )
                held["logits"] = jnp.where(allowed[:, None], logits, -1e30)
            if at == 3:
                logits = held.pop("logits")
                weights = jnp.exp(logits - jnp.max(logits, axis=-1, keepdims=True))
                held["soft"] = weights / jnp.sum(weights, axis=-1, keepdims=True)
                held["probs"] = held["soft"].astype(BF)
                held["attended"] = (
                    jnp.einsum(
                        "shqk,skd->sqhd",
                        held["probs"],
                        held["value"],
                        preferred_element_type=F32,
                    )
                    .reshape(rows, H * HD)
                    .astype(BF)
                )

        (w_qkv, w_out), ffn, cots = gather_weights(
            mv,
            [jnp.concatenate([q_weight, kv_weight, small], 1), out_weight],
            ffn,
            rounds - 2,
            cotangent,
            [mv.planes - 1, *range(rounds - 2, rounds + 3)],
            held,
            attention,
        )
        cots = [cotangent, *cots]
        w_query, w_keyval, small = split_qkv(w_qkv)
        gain_one, gain_two, bias_down = small[0], small[1], small[2]
        norm_one_b, query, key, value = (held[k] for k in ("norm_one", "query", "key", "value"))
        soft, probs, attended = (held[k] for k in ("soft", "probs", "attended"))
        ffn = lax.all_gather(ffn, "dp", axis=0, tiled=True, axis_index_groups=mv.squares())
        hidden_one = x_value + dot_nn(attended, w_out)
        norm_two_b = rms_scale(hidden_one, gain_two).astype(BF)

        order = [*range(1, mv.planes), 0]
        norms, cots, norm_pieces, cot_pieces = [norm_two_b], list(cots), [], []
        swap_early = [attended, norm_one_b]
        swapped = []

        def piece_work(step):
            gate = dot_nt(norm_pieces[step], w_gate) + b_gate
            up = dot_nt(norm_pieces[step], w_up) + b_up
            grad_act = dot_nt(cot_pieces[step], w_down)
            act, act_back = jax.vjp(glu_tanh, gate, up)
            grad_gate, grad_up = (v.astype(BF) for v in act_back(grad_act))
            partial = dot_nn(grad_gate, w_gate) + dot_nn(grad_up, w_up)
            return act.astype(BF), grad_gate, grad_up, partial[:rows], partial[rows:].astype(BF)

        acts, grads_all = [], ([], [])
        sends, received, parts, gots, partials = {}, None, {}, {}, None
        last = mv.planes + 1
        for at in range(last + 1):
            norms, cots, swap_early, norm_pieces, cot_pieces, acts, grads_all = fence(
                (norms, cots, swap_early, norm_pieces, cot_pieces, acts, grads_all)
            )
            if at == last:
                sends, norm_pieces, acts, grads_all = fence((sends, norm_pieces, acts, grads_all))
            if at == 1:
                ffn = ffn.reshape(4, 3 * padded, D)
                w_down, w_gate, w_up = (
                    ffn[:, i * padded : (i + 1) * padded].reshape(4 * padded, D) for i in range(3)
                )
                b_gate, b_up = (
                    ffn[:, padded + units + i, :padded].reshape(4 * padded).astype(F32)
                    for i in range(2)
                )
                w_down, w_gate, w_up, b_gate, b_up, norm_pieces = fence(
                    (w_down, w_gate, w_up, b_gate, b_up, norm_pieces)
                )
            if at <= mv.planes - 2:
                norms.append(mv.up(norms[at]))
            if 4 + at < mv.planes:
                cots.append(mv.up(cots[3 + at]))
            if at - 2 in sends:
                received = mv.up(sends.pop(at - 2))
            if at < mv.planes:
                norm_pieces.append(jnp.concatenate([norms[at], mv.other(norms[at])], 0))
                cot_pieces.append(jnp.concatenate([cots[at], mv.other(cots[at])], 0))
            if at in (0, mv.planes):
                early = swap_early[min(at, 1)]
                swapped.append(jnp.concatenate([early, mv.other(early)], 0))
            step = at - 1
            if 0 <= step < mv.planes:
                act, grad_gate, grad_up, own_part, their_part = piece_work(step)
                acts.append(act)
                grads_all[0].append(grad_gate)
                grads_all[1].append(grad_up)
                parts[step] = own_part
                gots[step] = mv.other(their_part)
            if at == last:
                acts = jnp.concatenate(acts, 0)
                grads_all = [jnp.concatenate(v, 0) for v in grads_all]
                cot_all = jnp.concatenate(cot_pieces, 0)
                norm_all = jnp.concatenate(norm_pieces, 0)
                partials = [dot_tn(acts, cot_all, BF)]
                partials += [dot_tn(v, norm_all, BF) for v in grads_all]
            (
                norms,
                cots,
                norm_pieces,
                cot_pieces,
                swapped,
                acts,
                grads_all,
                parts,
                gots,
                received,
                partials,
            ) = (
                fence(
                    (
                        norms,
                        cots,
                        norm_pieces,
                        cot_pieces,
                        swapped,
                        acts,
                        grads_all,
                        parts,
                        gots,
                        received,
                        partials,
                    )
                )
            )
            if step >= 1:
                done = step if step < mv.planes else 0
                total = parts.pop(done) + gots.pop(done).astype(F32)
                if received is not None:
                    total = total + received.astype(F32)
                    received = None
                if done:
                    sends[done] = total.astype(BF)
        grad_norm_two = total
        attended_both, norm_both = swapped
        ffn_sums = [
            lax.psum_scatter(
                v, "dp", scatter_dimension=0, tiled=True, axis_index_groups=mv.squares()
            )
            for v in partials
        ]

        _, norm_two_back = jax.vjp(rms_scale, hidden_one, gain_two)
        grad_rms_two, grad_gain_two = norm_two_back(grad_norm_two)
        grad_hidden = cotangent.astype(F32) + grad_rms_two
        grad_hidden_b = grad_hidden.astype(BF)

        out_partial = dot_tn(attended_both, core_half(mv, grad_hidden_b), BF)
        out_partial, grad_hidden_b, grads_all, acts = fence(
            (out_partial, grad_hidden_b, grads_all, acts)
        )
        held = {"grads": grads_all, "acts": acts}

        def scores_back(grad_attended):
            grad_probs = jnp.einsum(
                "sqhd,skd->shqk", grad_attended, value, preferred_element_type=F32
            )
            return (
                soft * (grad_probs - jnp.sum(grad_probs * soft, axis=-1, keepdims=True))
            ).astype(BF)

        def lin_back(grad_scores, grad_attended):
            grad_value = jnp.einsum(
                "shqk,sqhd->skd", probs, grad_attended, preferred_element_type=F32
            ).reshape(rows, HD)
            grad_query = jnp.einsum(
                "shqk,skd->sqhd", grad_scores, key, preferred_element_type=F32
            ).reshape(rows, H, HD)
            grad_key = jnp.einsum(
                "shqk,sqhd->skd", grad_scores, query, preferred_element_type=F32
            ).reshape(rows, HD)
            grad_kv_lin = jnp.concatenate(
                [rotate(grad_key, cosine, -sine), grad_value], 1
            ).astype(BF)
            grad_q_lin = (
                rotate(grad_query * head_scale, cosine[:, None, :], -sine[:, None, :])
                .reshape(rows, H * HD)
                .astype(BF)
            )
            return grad_q_lin, grad_kv_lin

        def work(at):
            if at == 0:
                grad_attended = dot_nt(grad_hidden_b, w_out).astype(BF)
                held["attended"] = grad_attended.reshape(seqs, LENGTH, H, HD)
                acts_two = held.pop("acts").reshape(mv.planes, 2, rows, 4 * padded)
                mine, theirs = (
                    dot_nn(acts_two[:, i].reshape(mv.planes * rows, 4 * padded), w_down)
                    .astype(BF)
                    .reshape(mv.planes, rows, D)
                    for i in (0, 1)
                )
                held["branch"], held["got"] = mine, mv.other(theirs)
            if at == 1:
                held["scores"] = scores_back(held["attended"])
            if at == 2:
                held["q"], held["kv"] = lin_back(held.pop("scores"), held.pop("attended"))
            if at == 3:
                half = jnp.concatenate([core_half(mv, held["q"]), core_half(mv, held["kv"])], 1)
                held["partial"] = dot_tn(norm_both, half, BF)
            if at == 4:
                grad_norm_one = dot_nt(held.pop("q"), w_query) + dot_nt(held.pop("kv"), w_keyval)
                _, norm_one_back = jax.vjp(rms_scale, x_value, gain_one)
                grad_rms_one, grad_gain_one = norm_one_back(grad_norm_one)
                held["input_grad"] = (grad_hidden + grad_rms_one).astype(BF)
                down_bias_sum = jnp.sum(cotangent, axis=0, dtype=F32)
                part = D // mv.n
                small = jnp.stack([grad_gain_one, grad_gain_two, down_bias_sum])
                small = small.reshape(3, mv.planes, 2, 2, 2, part).transpose(2, 3, 4, 1, 0, 5)
                held["small"] = small
                bias = jnp.stack([jnp.sum(v, axis=0, dtype=F32) for v in held.pop("grads")])
                bias = bias.reshape(2, 2, 2, padded)[..., :units]
                held["bias"] = bias.transpose(1, 2, 0, 3)
            for stage, (coordinate, move) in enumerate(
                ((mv.y, mv.over_y), (mv.x, mv.over_x), (mv.core, mv.other))
            ):
                if at == 5 + stage:
                    for name in ("small", "bias")[: 2 if stage < 2 else 1]:
                        whole = held[name]
                        keep = lax.dynamic_index_in_dim(whole, coordinate, 0, keepdims=False)
                        away = lax.dynamic_index_in_dim(whole, 1 - coordinate, 0, keepdims=False)
                        held[name] = keep + move(away)
            for step in range(1, mv.planes):
                if at == 8 + (step - 1) // 2:
                    away = lax.dynamic_index_in_dim(
                        held["small"], (mv.z + step) % mv.planes, 0, keepdims=False
                    )
                    held["small_sum"] = held.get("small_sum", 0.0) + mv.up(away, step)

            ring = at - 1
            if 0 <= ring < mv.planes:
                at_piece = order[ring]
                branch = held["branch"][at_piece].astype(F32) + held["got"][at_piece].astype(F32)
                if ring > 0:
                    branch = branch + held.pop("ring").astype(F32)
                if ring < mv.planes - 1:
                    held["ring"] = mv.up(branch.astype(BF))
                else:
                    held["output"] = (hidden_one + branch + bias_down).astype(BF)
            if at == mv.planes + 4:
                held["out_grad"] = jnp.concatenate(swap_halves(mv, held.pop("sum0")), 1)
                held["ffn"] = [v[:units].astype(F32) for v in ffn_sums]

        scatter_grads(
            mv, [lambda: out_partial, lambda: held.pop("partial")], D, held, work
        )
        small = held["small_sum"] + lax.dynamic_index_in_dim(
            held["small"], mv.z, 0, keepdims=False
        )
        down_grad, gate_grad, up_grad = held["ffn"]
        first, second = swap_halves(mv, held["sum1"])
        q_grad = jnp.concatenate([first[:, : D // 2], second[:, : D // 2]], 1)
        kv_grad = jnp.concatenate([first[:, D // 2 :], second[:, D // 2 :]], 1)

        return (
            held["output"],
            held["input_grad"],
            small[0],
            q_grad,
            kv_grad,
            held["out_grad"],
            small[1],
            gate_grad,
            held["bias"][0],
            up_grad,
            held["bias"][1],
            down_grad,
            small[2],
        )

    return body


def solution(mesh):
    matrix, vector = P("dp", None), P("dp")
    return jax.shard_map(
        make_body(mesh.shape["dp"]),
        mesh=mesh,
        in_specs=(
            matrix,
            vector,
            vector,
            matrix,
            matrix,
            matrix,
            vector,
            matrix,
            vector,
            matrix,
            vector,
            matrix,
            vector,
            matrix,
        ),
        out_specs=(
            matrix,
            matrix,
            vector,
            matrix,
            matrix,
            matrix,
            vector,
            matrix,
            vector,
            matrix,
            vector,
            matrix,
            vector,
        ),
        check_vma=False,
    )
```

```python
import functools

import jax
import jax.numpy as jnp
from jax import lax
from jax.experimental import pallas as pl
from jax.experimental.pallas import tpu as pltpu
from jax.experimental.layout import Layout, with_layout_constraint
from jax.sharding import PartitionSpec as P

D = 2560
H = 10
HD = 256
LENGTH = 256
F32 = jnp.float32
BF = jnp.bfloat16
EPS = 1e-06


ROWS = Layout((0, 1))


def row_major(value):
    return with_layout_constraint(value, ROWS)


def rms_scale(values, gain):
    return values * lax.rsqrt(jnp.mean(values * values, axis=-1, keepdims=True) + EPS) * gain


def angles(positions):
    quarter = HD // 4
    ladder = jnp.arange(quarter, dtype=F32)
    freq = 10000.0 ** (-2.0 * ladder / (HD // 2))
    angle = positions.astype(F32)[:, None] * freq[None, :]
    return (jnp.cos(angle), jnp.sin(angle))


def rotate(values, cosine, sine):
    quarter = cosine.shape[-1]
    first = values[..., :quarter]
    second = values[..., quarter : 2 * quarter]
    rest = values[..., 2 * quarter :]
    return jnp.concatenate(
        [first * cosine - second * sine, second * cosine + first * sine, rest], -1
    )


def dot_tn(left, right, out=F32):
    return lax.dot_general(
        left, right, (((0,), (0,)), ((), ())), preferred_element_type=F32
    ).astype(out)


def dot_nt(left, right):
    return lax.dot_general(left, right, (((1,), (1,)), ((), ())), preferred_element_type=F32)


def dot_nn(left, right):
    return jnp.dot(left, right, preferred_element_type=F32)


def glu_tanh(gate, up):
    return jax.nn.gelu(gate, approximate=True) * up


class Moves:
    def __init__(self, n):
        self.n = n
        self.planes = n // 8
        me = lax.axis_index("dp")
        self.core = me % 2
        self.x = (me // 2) % 2
        self.y = (me // 4) % 2
        self.z = me // 8

    def flip(self, value, bit):
        return lax.ppermute(value, "dp", [(i, i ^ bit) for i in range(self.n)])

    def other(self, value):
        return self.flip(value, 1)

    def over_x(self, value):
        return self.flip(value, 2)

    def over_y(self, value):
        return self.flip(value, 4)

    def lines(self):
        return [[z * 8 + at + core for z in range(self.planes) for core in (0, 1)] for at in (0, 2, 4, 6)]

    def squares(self):
        return [
            [z * 8 + at + core for at in (0, 2, 4, 6)]
            for z in range(self.planes)
            for core in (0, 1)
        ]

    def up(self, value, steps=1):
        return lax.ppermute(value, "dp", [(i, (i + 8 * steps) % self.n) for i in range(self.n)])


def fence(values):
    return lax.optimization_barrier(values)


def place_kernel(at_ref, mine, theirs, *refs):
    whole = refs[-1]

    @pl.when(pl.program_id(0) < 4)
    def _():
        whole[...] = mine[...]

    @pl.when(pl.program_id(0) >= 4)
    def _():
        whole[...] = theirs[...]


class Rows:
    def __init__(self, mv, rows, width, dtype):
        self.mv, self.rows = mv, rows
        self.shape = jax.ShapeDtypeStruct((mv.n * rows, width), dtype)
        self.whole = None

    def put(self, step, blocks):
        mv, rows = self.mv, self.rows
        z = (mv.z - step) % mv.planes
        at = [
            ((z * 2 + (mv.y ^ fy)) * 2 + (mv.x ^ fx)) * 2 + (mv.core ^ flip)
            for flip in (0, 1)
            for fy in (0, 1)
            for fx in (0, 1)
        ]
        if rows % 16:
            whole = self.whole
            if whole is None:
                whole = jnp.zeros(self.shape.shape, self.shape.dtype)
            for j in range(8):
                block = blocks[j // 4][(j % 4) * rows : (j % 4 + 1) * rows]
                whole = lax.dynamic_update_slice(whole, block, (at[j] * rows, 0))
            self.whole = whole
            return
        width = self.shape.shape[1]
        before = [] if self.whole is None else [self.whole]
        self.whole = pl.pallas_call(
            place_kernel,
            out_shape=self.shape,
            grid_spec=pltpu.PrefetchScalarGridSpec(
                num_scalar_prefetch=1,
                grid=(8,),
                in_specs=[
                    pl.BlockSpec((rows, width), lambda j, at: (jnp.minimum(j, 3), 0)),
                    pl.BlockSpec((rows, width), lambda j, at: (jnp.maximum(j - 4, 0), 0)),
                ]
                + [pl.BlockSpec(memory_space=pl.ANY)] * len(before),
                out_specs=pl.BlockSpec((rows, width), lambda j, at: (at[j], 0)),
            ),
            input_output_aliases={3: 0} if before else {},
            name="place_rows",
        )(jnp.stack(at).astype(jnp.int32), *blocks, *before)

    def done(self):
        return row_major(self.whole)


def gather_weights(mv, to_all, late, late_round, block, block_rounds, held, work):
    halves = [block[: block.shape[0] // 2], block[block.shape[0] // 2 :]]
    arrived = []
    rows = to_all[0].shape[0]
    half = rows // 2
    builders = [Rows(mv, rows, v.shape[1], v.dtype) for v in to_all]
    items = [(i, k) for i in range(len(to_all)) for k in range(mv.planes)]
    piece = list(to_all)
    first = second = whole = None
    starts = []
    for at in range(len(items) + 3):
        placed = [b.whole for b in builders]
        state = (piece, first, second, whole, halves, placed, held)
        if at <= late_round:
            late, state = fence((late, state))
        else:
            state = fence(state)
        piece, first, second, whole, halves, placed, now = state
        held.update(now)
        for builder, value in zip(builders, placed):
            builder.whole = value
        send_x, send_y = [], []
        new_first = new_second = new_whole = None
        fresh = at < len(items)
        if fresh:
            i, k = items[at]
            send_x.append(piece[i])
            send_y.append(piece[i])
        joined = fresh and first is not None and first[1].shape[1] == piece[i].shape[1]
        if first is not None:
            own, from_x, from_y = first
            diag_b, diag_a = from_y[half:rows], from_x[:half]
            if joined or not fresh:
                send_x.append(diag_b)
                send_y.append(diag_a)
            else:
                diag_b, diag_a = mv.over_x(diag_b), mv.over_y(diag_a)
        if send_x:
            got_x = mv.over_x(jnp.concatenate(send_x, 0))
            got_y = mv.over_y(jnp.concatenate(send_y, 0))
        if first is not None:
            if joined or not fresh:
                start = rows if fresh else 0
                diag_b, diag_a = got_x, got_y
            else:
                start = 0
            new_second = (own, from_x, from_y, diag_a, diag_b)
            starts.append(start)
        if fresh:
            new_first = (piece[i], got_x, got_y)
            if k < mv.planes - 1:
                piece[i] = mv.up(piece[i])
        if second is not None:
            own, from_x, from_y, diag_a, diag_b = second
            start = starts[at - 2]
            block = jnp.concatenate(
                [
                    own,
                    from_x[:rows],
                    from_y[:rows],
                    diag_a[start : start + half],
                    diag_b[start : start + half],
                ],
                0,
            )
            new_whole = (block, mv.other(block))
        if at in block_rounds:
            which = block_rounds.index(at) % 2
            halves[which] = mv.up(halves[which])
            arrived.append(halves[which])
        if whole is not None:
            i, k = items[at - 3]
            builders[i].put(k, whole)
        work(at - mv.planes - 3, placed[0])
        first, second, whole = new_first, new_second, new_whole
    arrived = [jnp.concatenate(arrived[i : i + 2], 0) for i in range(0, len(arrived), 2)]
    return [b.done() for b in builders], late, arrived


def mine_of(mv, value, axis=0):
    size = value.shape[axis] // 2
    return lax.dynamic_slice_in_dim(value, mv.core * size, size, axis)


def theirs_of(mv, value, axis=0):
    size = value.shape[axis] // 2
    return lax.dynamic_slice_in_dim(value, (1 - mv.core) * size, size, axis)


def swap_halves(mv, total):
    rows = total.shape[0] // 2
    mine = lax.dynamic_slice(total, (mv.core * rows, 0), (rows, total.shape[1]))
    theirs = mv.other(lax.dynamic_slice(total, ((1 - mv.core) * rows, 0), (rows, total.shape[1])))
    return jnp.where(mv.core == 0, mine, theirs), jnp.where(mv.core == 0, theirs, mine)


def core_half(mv, value):
    width = value.shape[1] // 2
    mine = jnp.where(mv.core == 0, value[:, :width], value[:, width:])
    theirs = jnp.where(mv.core == 0, value[:, width:], value[:, :width])
    return jnp.concatenate([mine, mv.other(theirs)], 0)


def make_body(n):
    def body(
        tokens,
        doc_positions,
        attn_gain,
        q_weight,
        kv_weight,
        out_weight,
        ffn_gain,
        gate_weight,
        gate_bias,
        up_weight,
        up_bias,
        down_weight,
        down_bias,
        cotangent,
    ):
        mv = Moves(n)
        head_scale = HD ** (-0.5)
        rows = tokens.shape[0]
        seqs = rows // LENGTH
        small = jnp.stack([attn_gain, ffn_gain, down_bias], 1)
        small = jnp.pad(small, ((0, 0), (0, 125)))
        units = gate_weight.shape[0]
        padded = -(-(units + 2) // 128) * 128

        def pad_rows(value):
            return jnp.pad(value, ((0, padded - units), (0, 0)))

        bias_rows = jnp.pad(
            jnp.stack([gate_bias, up_bias]), ((0, padded - units - 2), (0, D - units))
        )
        ffn = jnp.concatenate(
            [pad_rows(down_weight), gate_weight, bias_rows, pad_rows(up_weight)], 0
        )
        rounds = 2 * mv.planes
        x_value = tokens.astype(F32)
        cosine, sine = angles(doc_positions)
        index = jnp.arange(LENGTH)
        distance = index[:, None] - index[None, :]
        allowed = (distance[None] >= 0) & (
            distance[None] <= doc_positions.reshape(seqs, LENGTH)[:, :, None]
        )
        held = {}

        def split_qkv(w_qkv):
            small = w_qkv[:, D + 2 * HD :].T.astype(F32)
            return w_qkv[:, :D], w_qkv[:, D : D + 2 * HD], small

        def attention(at, w_qkv):
            if at == 1:
                w_query, w_keyval, small = split_qkv(w_qkv)
                norm_one_b = rms_scale(x_value, small[0]).astype(BF)
                held["norm_one"] = norm_one_b
                q_lin = dot_nn(norm_one_b, w_query).reshape(rows, H, HD)
                query = rotate(q_lin, cosine[:, None, :], sine[:, None, :]) * head_scale
                held["query"] = query.astype(BF).reshape(seqs, LENGTH, H, HD)
                held["kv"] = dot_nn(norm_one_b, w_keyval)
            if at == 2:
                kv_lin = held.pop("kv")
                key = rotate(kv_lin[:, :HD], cosine, sine).astype(BF)
                held["key"] = key.reshape(seqs, LENGTH, HD)
                held["value"] = kv_lin[:, HD:].astype(BF).reshape(seqs, LENGTH, HD)
                logits = jnp.einsum(
                    "sqhd,skd->shqk", held["query"], held["key"], preferred_element_type=F32
                )
                held["logits"] = jnp.where(allowed[:, None], logits, -1e30)
            if at == 3:
                logits = held.pop("logits")
                weights = jnp.exp(logits - jnp.max(logits, axis=-1, keepdims=True))
                held["soft"] = weights / jnp.sum(weights, axis=-1, keepdims=True)
                held["probs"] = held["soft"].astype(BF)
                held["attended"] = (
                    jnp.einsum(
                        "shqk,skd->sqhd",
                        held["probs"],
                        held["value"],
                        preferred_element_type=F32,
                    )
                    .reshape(rows, H * HD)
                    .astype(BF)
                )

        (w_qkv, w_out), ffn, cots = gather_weights(
            mv,
            [jnp.concatenate([q_weight, kv_weight, small], 1), out_weight],
            ffn,
            rounds - 2,
            cotangent,
            [mv.planes - 1, *range(rounds - 2, rounds + 3)],
            held,
            attention,
        )
        cots = [cotangent, *cots]
        w_query, w_keyval, small = split_qkv(w_qkv)
        gain_one, gain_two, bias_down = small[0], small[1], small[2]
        norm_one_b, query, key, value = (held[k] for k in ("norm_one", "query", "key", "value"))
        soft, probs, attended = (held[k] for k in ("soft", "probs", "attended"))
        ffn = lax.all_gather(ffn, "dp", axis=0, tiled=True, axis_index_groups=mv.squares())
        hidden_one = x_value + dot_nn(attended, w_out)
        norm_two_b = rms_scale(hidden_one, gain_two).astype(BF)

        order = [*range(1, mv.planes), 0]
        norms, cots, norm_pieces, cot_pieces = [norm_two_b], list(cots), [], []
        swap_early = [attended, norm_one_b]
        swapped = []

        def piece_work(step):
            gate = dot_nt(norm_pieces[step], w_gate) + b_gate
            up = dot_nt(norm_pieces[step], w_up) + b_up
            grad_act = dot_nt(cot_pieces[step], w_down)
            act, act_back = jax.vjp(glu_tanh, gate, up)
            grad_gate, grad_up = (v.astype(BF) for v in act_back(grad_act))
            partial = dot_nn(grad_gate, w_gate) + dot_nn(grad_up, w_up)
            return act.astype(BF), grad_gate, grad_up, partial[:rows], partial[rows:].astype(BF)

        acts, grads_all = [], ([], [])
        sends, received, parts, gots, partials = {}, None, {}, {}, None
        last = mv.planes + 1
        for at in range(last + 1):
            norms, cots, swap_early, norm_pieces, cot_pieces, acts, grads_all = fence(
                (norms, cots, swap_early, norm_pieces, cot_pieces, acts, grads_all)
            )
            if at == last:
                sends, norm_pieces, acts, grads_all = fence((sends, norm_pieces, acts, grads_all))
            if at == 1:
                ffn = ffn.reshape(4, 3 * padded, D)
                w_down, w_gate, w_up = (
                    ffn[:, i * padded : (i + 1) * padded].reshape(4 * padded, D) for i in range(3)
                )
                b_gate, b_up = (
                    ffn[:, padded + units + i, :padded].reshape(4 * padded).astype(F32)
                    for i in range(2)
                )
                w_down, w_gate, w_up, b_gate, b_up, norm_pieces = fence(
                    (w_down, w_gate, w_up, b_gate, b_up, norm_pieces)
                )
            if at <= mv.planes - 2:
                norms.append(mv.up(norms[at]))
            if 4 + at < mv.planes:
                cots.append(mv.up(cots[3 + at]))
            if at - 2 in sends:
                received = mv.up(sends.pop(at - 2))
            if at < mv.planes:
                norm_pieces.append(jnp.concatenate([norms[at], mv.other(norms[at])], 0))
                cot_pieces.append(jnp.concatenate([cots[at], mv.other(cots[at])], 0))
            if at in (0, mv.planes):
                early = swap_early[min(at, 1)]
                swapped.append(jnp.concatenate([early, mv.other(early)], 0))
            step = at - 1
            if 0 <= step < mv.planes:
                act, grad_gate, grad_up, own_part, their_part = piece_work(step)
                acts.append(act)
                grads_all[0].append(grad_gate)
                grads_all[1].append(grad_up)
                parts[step] = own_part
                gots[step] = mv.other(their_part)
            if at == last:
                acts = jnp.concatenate(acts, 0)
                grads_all = [jnp.concatenate(v, 0) for v in grads_all]
                cot_all = jnp.concatenate(cot_pieces, 0)
                norm_all = jnp.concatenate(norm_pieces, 0)
                acts_two = acts.reshape(mv.planes, 2, rows, 4 * padded)
                branch_mine, branch_other = (
                    dot_nn(acts_two[:, i].reshape(mv.planes * rows, 4 * padded), w_down)
                    .astype(BF)
                    .reshape(mv.planes, rows, D)
                    for i in (0, 1)
                )
                partials = (branch_mine, mv.other(branch_other), dot_tn(acts, cot_all, BF))
            (
                norms,
                cots,
                norm_pieces,
                cot_pieces,
                swapped,
                acts,
                grads_all,
                parts,
                gots,
                received,
                partials,
            ) = (
                fence(
                    (
                        norms,
                        cots,
                        norm_pieces,
                        cot_pieces,
                        swapped,
                        acts,
                        grads_all,
                        parts,
                        gots,
                        received,
                        partials,
                    )
                )
            )
            if step >= 1:
                done = step if step < mv.planes else 0
                total = parts.pop(done) + gots.pop(done).astype(F32)
                if received is not None:
                    total = total + received.astype(F32)
                    received = None
                if done:
                    sends[done] = total.astype(BF)
        grad_norm_two = total
        attended_both, norm_both = swapped
        branch_mine, branch_got, down_partial = partials

        def branch_step(ring, received):
            at_piece = order[ring]
            branch = branch_mine[at_piece].astype(F32) + branch_got[at_piece].astype(F32)
            return branch if received is None else branch + received.astype(F32)

        def ffn_sum(value):
            return lax.psum_scatter(
                value, "dp", scatter_dimension=0, tiled=True, axis_index_groups=mv.squares()
            )

        down_sum = ffn_sum(down_partial)
        branch_sent = branch_step(0, None).astype(BF)
        grad_norm_two, branch_sent = fence((grad_norm_two, branch_sent))
        branch_ring = mv.up(branch_sent)

        _, norm_two_back = jax.vjp(rms_scale, hidden_one, gain_two)
        grad_rms_two, grad_gain_two = norm_two_back(grad_norm_two)
        grad_hidden = cotangent.astype(F32) + grad_rms_two
        grad_hidden_b = grad_hidden.astype(BF)

        out_partial = dot_tn(attended_both, core_half(mv, grad_hidden_b), BF)
        out_partial, grad_hidden_b, grads_all, norm_all, branch_ring = fence(
            (out_partial, grad_hidden_b, grads_all, norm_all, branch_ring)
        )
        held = {"grads": grads_all, "norm": norm_all, "out": out_partial, "branch": branch_ring}

        def scores_back(grad_attended):
            grad_probs = jnp.einsum(
                "sqhd,skd->shqk", grad_attended, value, preferred_element_type=F32
            )
            return (
                soft * (grad_probs - jnp.sum(grad_probs * soft, axis=-1, keepdims=True))
            ).astype(BF)

        def lin_back(grad_scores, grad_attended):
            grad_value = jnp.einsum(
                "shqk,sqhd->skd", probs, grad_attended, preferred_element_type=F32
            ).reshape(rows, HD)
            grad_query = jnp.einsum(
                "shqk,skd->sqhd", grad_scores, key, preferred_element_type=F32
            ).reshape(rows, H, HD)
            grad_key = jnp.einsum(
                "shqk,sqhd->skd", grad_scores, query, preferred_element_type=F32
            ).reshape(rows, HD)
            grad_kv_lin = jnp.concatenate(
                [rotate(grad_key, cosine, -sine), grad_value], 1
            ).astype(BF)
            grad_q_lin = (
                rotate(grad_query * head_scale, cosine[:, None, :], -sine[:, None, :])
                .reshape(rows, H * HD)
                .astype(BF)
            )
            return grad_q_lin, grad_kv_lin

        chip = D // (n // 2)
        plane = 4 * chip

        class Scatter:
            def __init__(self, base, chip):
                self.base, self.chip, self.half, self.at = base, chip, chip // 2, 0

            def block(self, array, flip_y, flip_x, low=True, high=True):
                index = (mv.y ^ flip_y) * 2 + (mv.x ^ flip_x)
                start = self.base + index * self.chip + (0 if low else self.half)
                count = self.half * (low + high)
                return lax.dynamic_slice(array, (start, 0), (count, array.shape[1]))

            def open(self, array, send_x, send_y):
                send_x += [
                    self.block(array, 1, 1, high=False),
                    self.block(array, 0, 1, high=False),
                ]
                send_y += [
                    self.block(array, 1, 1, low=False),
                    self.block(array, 1, 0, low=False),
                ]

            def close(self, array, got, send_x, send_y):
                from_x, from_y = got
                self.at = sum(v.shape[0] for v in send_x)
                last_x = self.block(array, 0, 1, low=False).astype(F32)
                last_y = self.block(array, 1, 0, high=False).astype(F32)
                send_x.append((last_x + from_y[: self.half].astype(F32)).astype(BF))
                send_y.append((last_y + from_x[: self.half].astype(F32)).astype(BF))

            def total(self, array, got, more):
                (from_x, from_y), (more_x, more_y) = got, more
                last = slice(self.at, self.at + self.half)
                kept = slice(self.half, self.chip)
                sums = self.block(array, 0, 0).astype(F32)
                sums += jnp.concatenate([from_x[kept], more_x[last]], 0).astype(F32)
                sums += jnp.concatenate([more_y[last], from_y[kept]], 0).astype(F32)
                return sums

        def exchange(send_x, send_y):
            if not send_x:
                return None
            send_x, send_y, now = fence(
                (jnp.concatenate(send_x, 0), jnp.concatenate(send_y, 0), held)
            )
            held.update(now)
            return mv.over_x(send_x), mv.over_y(send_y)

        planes = mv.planes
        lin_items = [Scatter(((mv.z - k) % planes) * plane, chip) for k in [*range(1, planes), 0]]
        out_item = Scatter(0, chip)
        ffn_items = [Scatter(0, padded), Scatter(0, padded)]
        open_lin, open_out = 2, max(4, planes)
        last_round = max(open_lin + planes + 1, open_out + 2, 6 + (planes - 2) // 3, 2 * planes - 3)
        for at in range(last_round + 1):
            now = fence(held)
            held.update(now)
            send_x, send_y = [], []
            j = at - open_lin
            if 0 <= j < planes:
                lin_items[j].open(held["lin"], send_x, send_y)
            if 0 <= j - 1 < planes:
                lin_items[j - 1].close(held["lin"], held["lin1"], send_x, send_y)
            out_x, out_y = [], []
            if at == open_out:
                out_item.open(held["out_b"], out_x, out_y)
            if at == open_out + 1:
                out_item.close(held["out_b"], held["out1"], out_x, out_y)
            ffn_x, ffn_y = [], []
            f = at - 1
            if 0 <= f < 2:
                ffn_items[f].open(held["partials"][f], ffn_x, ffn_y)
            if 0 <= f - 1 < 2:
                ffn_items[f - 1].close(held["partials"][f - 1], held["ffn1"], ffn_x, ffn_y)
            got, got_out = exchange(send_x, send_y), exchange(out_x, out_y)
            got_ffn = exchange(ffn_x, ffn_y)
            if at < planes - 1:
                z = (mv.z - at - 1) % planes
                rows_out = lax.dynamic_slice(held["out"], (z * plane, 0), (plane, D // 2))
                if at > 0:
                    rows_out = rows_out.astype(F32) + held.pop("out_ring").astype(F32)
                held["out_ring"] = mv.up(rows_out.astype(BF))
            if at == planes - 1:
                rows_out = lax.dynamic_slice(held.pop("out"), (mv.z * plane, 0), (plane, D // 2))
                rows_out = rows_out.astype(F32) + held.pop("out_ring").astype(F32)
                held["out_b"] = rows_out.astype(BF)
            ring = at - (planes - 1) + 1
            if 1 <= ring < planes:
                branch = branch_step(ring, held.pop("branch"))
                if ring < planes - 1:
                    held["branch"] = mv.up(branch.astype(BF))
                else:
                    held["output"] = (hidden_one + branch + bias_down).astype(BF)
            if 0 <= j - 2 < planes:
                sums = lin_items[j - 2].total(held["lin"], held["lin2"], held["lin1"])
                if j - 2 > 0:
                    sums = sums + held.pop("lin_ring").astype(F32)
                if j - 2 < planes - 1:
                    held["lin_ring"] = mv.up(sums.astype(BF))
                else:
                    held["lin_sum"] = sums
            if at == open_out + 2:
                sums = out_item.total(held["out_b"], held["out2"], held["out1"])
                held["out_grad"] = jnp.concatenate(swap_halves(mv, sums), 1)
            if 0 <= f - 2 < 2:
                sums = ffn_items[f - 2].total(
                    held["partials"][f - 2], held["ffn2"], held["ffn1"]
                )
                held[f"unit_grad{f - 2}"] = sums[:units]
            for one, two, new in (("ffn1", "ffn2", got_ffn),):
                if one in held:
                    held[two] = held.pop(one)
                if new is not None:
                    held[one] = new
            if "lin1" in held:
                held["lin2"] = held.pop("lin1")
            if got is not None:
                held["lin1"] = got
            if "out1" in held:
                held["out2"] = held.pop("out1")
            if got_out is not None:
                held["out1"] = got_out
            if at == 0:
                held["down_sum"] = down_sum
                partials = [dot_tn(v, held["norm"], BF) for v in held["grads"]]
                held["partials"] = partials
            if at == 1:
                grad_attended = dot_nt(grad_hidden_b, w_out).astype(BF)
                grad_attended = grad_attended.reshape(seqs, LENGTH, H, HD)
                held["q"], held["kv"] = lin_back(scores_back(grad_attended), grad_attended)
            if at == 1:
                both = jnp.concatenate([core_half(mv, held["q"]), core_half(mv, held["kv"])], 1)
                held["lin"] = dot_tn(norm_both, both, BF)
            if at == 2:
                grad_norm_one = dot_nt(held.pop("q"), w_query) + dot_nt(held.pop("kv"), w_keyval)
                _, norm_one_back = jax.vjp(rms_scale, x_value, gain_one)
                grad_rms_one, grad_gain_one = norm_one_back(grad_norm_one)
                held["input_grad"] = (grad_hidden + grad_rms_one).astype(BF)
                down_bias_sum = jnp.sum(cotangent, axis=0, dtype=F32)
                part = D // n
                small = jnp.stack([grad_gain_one, grad_gain_two, down_bias_sum])
                small = small.reshape(3, planes, 2, 2, 2, part).transpose(2, 3, 4, 1, 0, 5)
                held["small"] = small
                bias = jnp.stack([jnp.sum(v, axis=0, dtype=F32) for v in held.pop("grads")])
                bias = bias.reshape(2, 2, 2, padded)[..., :units]
                held["bias"] = bias.transpose(1, 2, 0, 3)
            for stage, (coordinate, move) in enumerate(
                ((mv.y, mv.over_y), (mv.x, mv.over_x), (mv.core, mv.other))
            ):
                if at == 3 + stage:
                    for name in ("small", "bias")[: 2 if stage < 2 else 1]:
                        whole = held[name]
                        keep = lax.dynamic_index_in_dim(whole, coordinate, 0, keepdims=False)
                        away = lax.dynamic_index_in_dim(whole, 1 - coordinate, 0, keepdims=False)
                        held[name] = keep + move(away)
            for step in range(1, planes):
                if at == min(6 + (step - 1) // 3, last_round):
                    away = lax.dynamic_index_in_dim(
                        held["small"], (mv.z + step) % planes, 0, keepdims=False
                    )
                    held["small_sum"] = held.get("small_sum", 0.0) + mv.up(away, step)
            if at == last_round - 1:
                held["down_grad"] = held.pop("down_sum")[:units].astype(F32)

        small = held["small_sum"] + lax.dynamic_index_in_dim(
            held["small"], mv.z, 0, keepdims=False
        )
        down_grad, gate_grad, up_grad = (
            held[k] for k in ("down_grad", "unit_grad0", "unit_grad1")
        )
        first, second = swap_halves(mv, held["lin_sum"])
        q_grad = jnp.concatenate([first[:, : D // 2], second[:, : D // 2]], 1)
        kv_grad = jnp.concatenate([first[:, D // 2 :], second[:, D // 2 :]], 1)

        return (
            held["output"],
            held["input_grad"],
            small[0],
            q_grad,
            kv_grad,
            held["out_grad"],
            small[1],
            gate_grad,
            held["bias"][0],
            up_grad,
            held["bias"][1],
            down_grad,
            small[2],
        )

    return body


def solution(mesh):
    matrix, vector = P("dp", None), P("dp")
    return jax.shard_map(
        make_body(mesh.shape["dp"]),
        mesh=mesh,
        in_specs=(
            matrix,
            vector,
            vector,
            matrix,
            matrix,
            matrix,
            vector,
            matrix,
            vector,
            matrix,
            vector,
            matrix,
            vector,
            matrix,
        ),
        out_specs=(
            matrix,
            matrix,
            vector,
            matrix,
            matrix,
            matrix,
            vector,
            matrix,
            vector,
            matrix,
            vector,
            matrix,
            vector,
        ),
        check_vma=False,
    )
```

```python
import functools

import jax
import jax.numpy as jnp
from jax import lax
from jax.experimental import pallas as pl
from jax.experimental.pallas import tpu as pltpu
from jax.experimental.layout import Layout, with_layout_constraint
from jax.sharding import PartitionSpec as P

D = 2560
H = 10
HD = 256
LENGTH = 256
F32 = jnp.float32
BF = jnp.bfloat16
EPS = 1e-06


ROWS = Layout((0, 1))


def row_major(value):
    return with_layout_constraint(value, ROWS)


def rms_scale(values, gain):
    return values * lax.rsqrt(jnp.mean(values * values, axis=-1, keepdims=True) + EPS) * gain


def angles(positions):
    quarter = HD // 4
    ladder = jnp.arange(quarter, dtype=F32)
    freq = 10000.0 ** (-2.0 * ladder / (HD // 2))
    angle = positions.astype(F32)[:, None] * freq[None, :]
    return (jnp.cos(angle), jnp.sin(angle))


def rotate(values, cosine, sine):
    quarter = cosine.shape[-1]
    first = values[..., :quarter]
    second = values[..., quarter : 2 * quarter]
    rest = values[..., 2 * quarter :]
    return jnp.concatenate(
        [first * cosine - second * sine, second * cosine + first * sine, rest], -1
    )


def dot_tn(left, right, out=F32):
    return lax.dot_general(
        left, right, (((0,), (0,)), ((), ())), preferred_element_type=F32
    ).astype(out)


def dot_nt(left, right):
    return lax.dot_general(left, right, (((1,), (1,)), ((), ())), preferred_element_type=F32)


def dot_nn(left, right):
    return jnp.dot(left, right, preferred_element_type=F32)


def glu_tanh(gate, up):
    return jax.nn.gelu(gate, approximate=True) * up


class Moves:
    def __init__(self, n):
        self.n = n
        self.planes = n // 8
        me = lax.axis_index("dp")
        self.core = me % 2
        self.x = (me // 2) % 2
        self.y = (me // 4) % 2
        self.z = me // 8

    def flip(self, value, bit):
        return lax.ppermute(value, "dp", [(i, i ^ bit) for i in range(self.n)])

    def other(self, value):
        return self.flip(value, 1)

    def over_x(self, value):
        return self.flip(value, 2)

    def over_y(self, value):
        return self.flip(value, 4)

    def lines(self):
        return [[z * 8 + at + core for z in range(self.planes) for core in (0, 1)] for at in (0, 2, 4, 6)]

    def squares(self):
        return [
            [z * 8 + at + core for at in (0, 2, 4, 6)]
            for z in range(self.planes)
            for core in (0, 1)
        ]

    def up(self, value, steps=1):
        return lax.ppermute(value, "dp", [(i, (i + 8 * steps) % self.n) for i in range(self.n)])


def fence(values):
    return lax.optimization_barrier(values)


def place_kernel(at_ref, mine, theirs, *refs):
    whole = refs[-1]

    @pl.when(pl.program_id(0) < 4)
    def _():
        whole[...] = mine[...]

    @pl.when(pl.program_id(0) >= 4)
    def _():
        whole[...] = theirs[...]


class Rows:
    def __init__(self, mv, rows, width, dtype):
        self.mv, self.rows = mv, rows
        self.shape = jax.ShapeDtypeStruct((mv.n * rows, width), dtype)
        self.whole = None

    def put(self, step, blocks):
        mv, rows = self.mv, self.rows
        z = (mv.z - step) % mv.planes
        at = [
            ((z * 2 + (mv.y ^ fy)) * 2 + (mv.x ^ fx)) * 2 + (mv.core ^ flip)
            for flip in (0, 1)
            for fy in (0, 1)
            for fx in (0, 1)
        ]
        if rows % 16:
            whole = self.whole
            if whole is None:
                whole = jnp.zeros(self.shape.shape, self.shape.dtype)
            for j in range(8):
                block = blocks[j // 4][(j % 4) * rows : (j % 4 + 1) * rows]
                whole = lax.dynamic_update_slice(whole, block, (at[j] * rows, 0))
            self.whole = whole
            return
        width = self.shape.shape[1]
        before = [] if self.whole is None else [self.whole]
        self.whole = pl.pallas_call(
            place_kernel,
            out_shape=self.shape,
            grid_spec=pltpu.PrefetchScalarGridSpec(
                num_scalar_prefetch=1,
                grid=(8,),
                in_specs=[
                    pl.BlockSpec((rows, width), lambda j, at: (jnp.minimum(j, 3), 0)),
                    pl.BlockSpec((rows, width), lambda j, at: (jnp.maximum(j - 4, 0), 0)),
                ]
                + [pl.BlockSpec(memory_space=pl.ANY)] * len(before),
                out_specs=pl.BlockSpec((rows, width), lambda j, at: (at[j], 0)),
            ),
            input_output_aliases={3: 0} if before else {},
            name="place_rows",
        )(jnp.stack(at).astype(jnp.int32), *blocks, *before)

    def done(self):
        return row_major(self.whole)


def gather_weights(mv, to_all, late, late_round, block, block_rounds, held, work):
    halves = [block[: block.shape[0] // 2], block[block.shape[0] // 2 :]]
    arrived = []
    rows = to_all[0].shape[0]
    half = rows // 2
    builders = [Rows(mv, rows, v.shape[1], v.dtype) for v in to_all]
    items = [(i, k) for i in range(len(to_all)) for k in range(mv.planes)]
    piece = list(to_all)
    first = second = whole = None
    starts = []
    for at in range(len(items) + 3):
        placed = [b.whole for b in builders]
        state = (piece, first, second, whole, halves, placed, held)
        if at <= late_round:
            late, state = fence((late, state))
        else:
            state = fence(state)
        piece, first, second, whole, halves, placed, now = state
        held.update(now)
        for builder, value in zip(builders, placed):
            builder.whole = value
        send_x, send_y = [], []
        new_first = new_second = new_whole = None
        fresh = at < len(items)
        if fresh:
            i, k = items[at]
            send_x.append(piece[i])
            send_y.append(piece[i])
        joined = fresh and first is not None and first[1].shape[1] == piece[i].shape[1]
        if first is not None:
            own, from_x, from_y = first
            diag_b, diag_a = from_y[half:rows], from_x[:half]
            if joined or not fresh:
                send_x.append(diag_b)
                send_y.append(diag_a)
            else:
                diag_b, diag_a = mv.over_x(diag_b), mv.over_y(diag_a)
        if send_x:
            got_x = mv.over_x(jnp.concatenate(send_x, 0))
            got_y = mv.over_y(jnp.concatenate(send_y, 0))
        if first is not None:
            if joined or not fresh:
                start = rows if fresh else 0
                diag_b, diag_a = got_x, got_y
            else:
                start = 0
            new_second = (own, from_x, from_y, diag_a, diag_b)
            starts.append(start)
        if fresh:
            new_first = (piece[i], got_x, got_y)
            if k < mv.planes - 1:
                piece[i] = mv.up(piece[i])
        if second is not None:
            own, from_x, from_y, diag_a, diag_b = second
            start = starts[at - 2]
            block = jnp.concatenate(
                [
                    own,
                    from_x[:rows],
                    from_y[:rows],
                    diag_a[start : start + half],
                    diag_b[start : start + half],
                ],
                0,
            )
            new_whole = (block, mv.other(block))
        if at in block_rounds:
            which = block_rounds.index(at) % 2
            halves[which] = mv.up(halves[which])
            arrived.append(halves[which])
        if whole is not None:
            i, k = items[at - 3]
            builders[i].put(k, whole)
        work(at - mv.planes - 3, placed[0])
        first, second, whole = new_first, new_second, new_whole
    arrived = [jnp.concatenate(arrived[i : i + 2], 0) for i in range(0, len(arrived), 2)]
    return [b.done() for b in builders], late, arrived


def mine_of(mv, value, axis=0):
    size = value.shape[axis] // 2
    return lax.dynamic_slice_in_dim(value, mv.core * size, size, axis)


def theirs_of(mv, value, axis=0):
    size = value.shape[axis] // 2
    return lax.dynamic_slice_in_dim(value, (1 - mv.core) * size, size, axis)


def swap_halves(mv, total):
    rows = total.shape[0] // 2
    mine = lax.dynamic_slice(total, (mv.core * rows, 0), (rows, total.shape[1]))
    theirs = mv.other(lax.dynamic_slice(total, ((1 - mv.core) * rows, 0), (rows, total.shape[1])))
    return jnp.where(mv.core == 0, mine, theirs), jnp.where(mv.core == 0, theirs, mine)


def core_half(mv, value):
    width = value.shape[1] // 2
    mine = jnp.where(mv.core == 0, value[:, :width], value[:, width:])
    theirs = jnp.where(mv.core == 0, value[:, width:], value[:, :width])
    return jnp.concatenate([mine, mv.other(theirs)], 0)


def make_body(n):
    def body(
        tokens,
        doc_positions,
        attn_gain,
        q_weight,
        kv_weight,
        out_weight,
        ffn_gain,
        gate_weight,
        gate_bias,
        up_weight,
        up_bias,
        down_weight,
        down_bias,
        cotangent,
    ):
        mv = Moves(n)
        head_scale = HD ** (-0.5)
        rows = tokens.shape[0]
        seqs = rows // LENGTH
        small = jnp.stack([attn_gain, ffn_gain, down_bias], 1)
        small = jnp.pad(small, ((0, 0), (0, 125)))
        units = gate_weight.shape[0]
        padded = -(-(units + 2) // 128) * 128

        def pad_rows(value):
            return jnp.pad(value, ((0, padded - units), (0, 0)))

        bias_rows = jnp.pad(
            jnp.stack([gate_bias, up_bias]), ((0, padded - units - 2), (0, D - units))
        )
        ffn = jnp.concatenate(
            [pad_rows(down_weight), gate_weight, bias_rows, pad_rows(up_weight)], 0
        )
        rounds = 2 * mv.planes
        x_value = tokens.astype(F32)
        cosine, sine = angles(doc_positions)
        index = jnp.arange(LENGTH)
        distance = index[:, None] - index[None, :]
        allowed = (distance[None] >= 0) & (
            distance[None] <= doc_positions.reshape(seqs, LENGTH)[:, :, None]
        )
        held = {}

        def split_qkv(w_qkv):
            small = w_qkv[:, D + 2 * HD :].T.astype(F32)
            return w_qkv[:, :D], w_qkv[:, D : D + 2 * HD], small

        def attention(at, w_qkv):
            if at == 1:
                w_query, w_keyval, small = split_qkv(w_qkv)
                norm_one_b = rms_scale(x_value, small[0]).astype(BF)
                held["norm_one"] = norm_one_b
                q_lin = dot_nn(norm_one_b, w_query).reshape(rows, H, HD)
                query = rotate(q_lin, cosine[:, None, :], sine[:, None, :]) * head_scale
                held["query"] = query.astype(BF).reshape(seqs, LENGTH, H, HD)
                held["kv"] = dot_nn(norm_one_b, w_keyval)
            if at == 2:
                kv_lin = held.pop("kv")
                key = rotate(kv_lin[:, :HD], cosine, sine).astype(BF)
                held["key"] = key.reshape(seqs, LENGTH, HD)
                held["value"] = kv_lin[:, HD:].astype(BF).reshape(seqs, LENGTH, HD)
                logits = jnp.einsum(
                    "sqhd,skd->shqk", held["query"], held["key"], preferred_element_type=F32
                )
                held["logits"] = jnp.where(allowed[:, None], logits, -1e30)
            if at == 3:
                logits = held.pop("logits")
                weights = jnp.exp(logits - jnp.max(logits, axis=-1, keepdims=True))
                held["soft"] = weights / jnp.sum(weights, axis=-1, keepdims=True)
                held["probs"] = held["soft"].astype(BF)
                held["attended"] = (
                    jnp.einsum(
                        "shqk,skd->sqhd",
                        held["probs"],
                        held["value"],
                        preferred_element_type=F32,
                    )
                    .reshape(rows, H * HD)
                    .astype(BF)
                )

        (w_qkv, w_out), ffn, cots = gather_weights(
            mv,
            [jnp.concatenate([q_weight, kv_weight, small], 1), out_weight],
            ffn,
            rounds - 2,
            cotangent,
            [mv.planes - 1, *range(rounds - 2, rounds + 3)],
            held,
            attention,
        )
        cots = [cotangent, *cots]
        w_query, w_keyval, small = split_qkv(w_qkv)
        gain_one, gain_two, bias_down = small[0], small[1], small[2]
        norm_one_b, query, key, value = (held[k] for k in ("norm_one", "query", "key", "value"))
        soft, probs, attended = (held[k] for k in ("soft", "probs", "attended"))
        ffn = lax.all_gather(ffn, "dp", axis=0, tiled=True, axis_index_groups=mv.squares())
        hidden_one = x_value + dot_nn(attended, w_out)
        norm_two_b = rms_scale(hidden_one, gain_two).astype(BF)

        order = [*range(1, mv.planes), 0]
        norms, cots, norm_pieces, cot_pieces = [norm_two_b], list(cots), [], []
        swap_early = [attended, norm_one_b]
        swapped = []

        def piece_work(step):
            gate = dot_nt(norm_pieces[step], w_gate) + b_gate
            up = dot_nt(norm_pieces[step], w_up) + b_up
            grad_act = dot_nt(cot_pieces[step], w_down)
            act, act_back = jax.vjp(glu_tanh, gate, up)
            grad_gate, grad_up = (v.astype(BF) for v in act_back(grad_act))
            partial = dot_nn(grad_gate, w_gate) + dot_nn(grad_up, w_up)
            return act.astype(BF), grad_gate, grad_up, partial[:rows], partial[rows:].astype(BF)

        acts, grads_all = [], ([], [])
        sends, received, parts, gots, partials = {}, None, {}, {}, None
        last = mv.planes + 1
        for at in range(last + 1):
            norms, cots, swap_early, norm_pieces, cot_pieces, acts, grads_all = fence(
                (norms, cots, swap_early, norm_pieces, cot_pieces, acts, grads_all)
            )
            if at == last:
                sends, norm_pieces, acts, grads_all = fence((sends, norm_pieces, acts, grads_all))
            if at == 1:
                ffn = ffn.reshape(4, 3 * padded, D)
                w_down, w_gate, w_up = (
                    ffn[:, i * padded : (i + 1) * padded].reshape(4 * padded, D) for i in range(3)
                )
                b_gate, b_up = (
                    ffn[:, padded + units + i, :padded].reshape(4 * padded).astype(F32)
                    for i in range(2)
                )
                w_down, w_gate, w_up, b_gate, b_up, norm_pieces = fence(
                    (w_down, w_gate, w_up, b_gate, b_up, norm_pieces)
                )
            if at <= mv.planes - 2:
                norms.append(mv.up(norms[at]))
            if 4 + at < mv.planes:
                cots.append(mv.up(cots[3 + at]))
            if at - 2 in sends:
                received = mv.up(sends.pop(at - 2))
            if at < mv.planes:
                norm_pieces.append(jnp.concatenate([norms[at], mv.other(norms[at])], 0))
                cot_pieces.append(jnp.concatenate([cots[at], mv.other(cots[at])], 0))
            if at in (0, mv.planes):
                early = swap_early[min(at, 1)]
                swapped.append(jnp.concatenate([early, mv.other(early)], 0))
            step = at - 1
            if 0 <= step < mv.planes:
                act, grad_gate, grad_up, own_part, their_part = piece_work(step)
                acts.append(act)
                grads_all[0].append(grad_gate)
                grads_all[1].append(grad_up)
                parts[step] = own_part
                gots[step] = mv.other(their_part)
            if at == last:
                acts = jnp.concatenate(acts, 0)
                grads_all = [jnp.concatenate(v, 0) for v in grads_all]
                cot_all = jnp.concatenate(cot_pieces, 0)
                norm_all = jnp.concatenate(norm_pieces, 0)
                acts_two = acts.reshape(mv.planes, 2, rows, 4 * padded)
                branch_mine, branch_other = (
                    dot_nn(acts_two[:, i].reshape(mv.planes * rows, 4 * padded), w_down)
                    .astype(BF)
                    .reshape(mv.planes, rows, D)
                    for i in (0, 1)
                )
                partials = (branch_mine, mv.other(branch_other), dot_tn(acts, cot_all, BF))
            (
                norms,
                cots,
                norm_pieces,
                cot_pieces,
                swapped,
                acts,
                grads_all,
                parts,
                gots,
                received,
                partials,
            ) = (
                fence(
                    (
                        norms,
                        cots,
                        norm_pieces,
                        cot_pieces,
                        swapped,
                        acts,
                        grads_all,
                        parts,
                        gots,
                        received,
                        partials,
                    )
                )
            )
            if step >= 1:
                done = step if step < mv.planes else 0
                total = parts.pop(done) + gots.pop(done).astype(F32)
                if received is not None:
                    total = total + received.astype(F32)
                    received = None
                if done:
                    sends[done] = total.astype(BF)
        grad_norm_two = total
        attended_both, norm_both = swapped
        branch_mine, branch_got, down_partial = partials

        def branch_step(ring, received):
            at_piece = order[ring]
            branch = branch_mine[at_piece].astype(F32) + branch_got[at_piece].astype(F32)
            return branch if received is None else branch + received.astype(F32)

        def ffn_sum(value):
            return lax.psum_scatter(
                value, "dp", scatter_dimension=0, tiled=True, axis_index_groups=mv.squares()
            )

        down_sum = ffn_sum(down_partial)
        branch_sent = branch_step(0, None).astype(BF)
        grad_norm_two, branch_sent = fence((grad_norm_two, branch_sent))
        branch_ring = mv.up(branch_sent)

        _, norm_two_back = jax.vjp(rms_scale, hidden_one, gain_two)
        grad_rms_two, grad_gain_two = norm_two_back(grad_norm_two)
        grad_hidden = cotangent.astype(F32) + grad_rms_two
        grad_hidden_b = grad_hidden.astype(BF)

        out_partial = dot_tn(attended_both, core_half(mv, grad_hidden_b), BF)
        grad_attended = dot_nt(grad_hidden_b, w_out).astype(BF)
        out_partial, grad_attended, grads_all, norm_all, branch_ring = fence(
            (out_partial, grad_attended, grads_all, norm_all, branch_ring)
        )
        held = {"attended": grad_attended, "grads": grads_all, "norm": norm_all, "out": out_partial, "branch": branch_ring}

        def scores_back(grad_attended):
            grad_probs = jnp.einsum(
                "sqhd,skd->shqk", grad_attended, value, preferred_element_type=F32
            )
            return (
                soft * (grad_probs - jnp.sum(grad_probs * soft, axis=-1, keepdims=True))
            ).astype(BF)

        def lin_back(grad_scores, grad_attended):
            grad_value = jnp.einsum(
                "shqk,sqhd->skd", probs, grad_attended, preferred_element_type=F32
            ).reshape(rows, HD)
            grad_query = jnp.einsum(
                "shqk,skd->sqhd", grad_scores, key, preferred_element_type=F32
            ).reshape(rows, H, HD)
            grad_key = jnp.einsum(
                "shqk,sqhd->skd", grad_scores, query, preferred_element_type=F32
            ).reshape(rows, HD)
            grad_kv_lin = jnp.concatenate(
                [rotate(grad_key, cosine, -sine), grad_value], 1
            ).astype(BF)
            grad_q_lin = (
                rotate(grad_query * head_scale, cosine[:, None, :], -sine[:, None, :])
                .reshape(rows, H * HD)
                .astype(BF)
            )
            return grad_q_lin, grad_kv_lin

        chip = D // (n // 2)
        plane = 4 * chip

        class Scatter:
            def __init__(self, base, chip):
                self.base, self.chip, self.half, self.at = base, chip, chip // 2, 0

            def block(self, array, flip_y, flip_x, low=True, high=True):
                index = (mv.y ^ flip_y) * 2 + (mv.x ^ flip_x)
                start = self.base + index * self.chip + (0 if low else self.half)
                count = self.half * (low + high)
                return lax.dynamic_slice(array, (start, 0), (count, array.shape[1]))

            def open(self, array, send_x, send_y):
                send_x += [
                    self.block(array, 1, 1, high=False),
                    self.block(array, 0, 1, high=False),
                ]
                send_y += [
                    self.block(array, 1, 1, low=False),
                    self.block(array, 1, 0, low=False),
                ]

            def close(self, array, got, send_x, send_y):
                from_x, from_y = got
                self.at = sum(v.shape[0] for v in send_x)
                last_x = self.block(array, 0, 1, low=False).astype(F32)
                last_y = self.block(array, 1, 0, high=False).astype(F32)
                send_x.append((last_x + from_y[: self.half].astype(F32)).astype(BF))
                send_y.append((last_y + from_x[: self.half].astype(F32)).astype(BF))

            def total(self, array, got, more):
                (from_x, from_y), (more_x, more_y) = got, more
                last = slice(self.at, self.at + self.half)
                kept = slice(self.half, self.chip)
                sums = self.block(array, 0, 0).astype(F32)
                sums += jnp.concatenate([from_x[kept], more_x[last]], 0).astype(F32)
                sums += jnp.concatenate([more_y[last], from_y[kept]], 0).astype(F32)
                return sums

        def exchange(send_x, send_y):
            if not send_x:
                return None
            send_x, send_y, now = fence(
                (jnp.concatenate(send_x, 0), jnp.concatenate(send_y, 0), held)
            )
            held.update(now)
            return mv.over_x(send_x), mv.over_y(send_y)

        planes = mv.planes
        lin_items = [Scatter(((mv.z - k) % planes) * plane, chip) for k in [*range(1, planes), 0]]
        out_item = Scatter(0, chip)
        ffn_items = [Scatter(0, padded), Scatter(0, padded)]
        open_lin, open_out = 2, max(4, planes)
        last_round = max(open_lin + planes + 1, open_out + 2, 6 + (planes - 2) // 3, 2 * planes - 3)
        for at in range(last_round + 1):
            now = fence(held)
            held.update(now)
            send_x, send_y = [], []
            j = at - open_lin
            if 0 <= j < planes:
                lin_items[j].open(held["lin"], send_x, send_y)
            if 0 <= j - 1 < planes:
                lin_items[j - 1].close(held["lin"], held["lin1"], send_x, send_y)
            out_x, out_y = [], []
            if at == open_out:
                out_item.open(held["out_b"], out_x, out_y)
            if at == open_out + 1:
                out_item.close(held["out_b"], held["out1"], out_x, out_y)
            ffn_x, ffn_y = [], []
            f = at - 1
            if 0 <= f < 2:
                ffn_items[f].open(held["partials"][f], ffn_x, ffn_y)
            if 0 <= f - 1 < 2:
                ffn_items[f - 1].close(held["partials"][f - 1], held["ffn1"], ffn_x, ffn_y)
            got, got_out = exchange(send_x, send_y), exchange(out_x, out_y)
            got_ffn = exchange(ffn_x, ffn_y)
            if at < planes - 1:
                z = (mv.z - at - 1) % planes
                rows_out = lax.dynamic_slice(held["out"], (z * plane, 0), (plane, D // 2))
                if at > 0:
                    rows_out = rows_out.astype(F32) + held.pop("out_ring").astype(F32)
                held["out_ring"] = mv.up(rows_out.astype(BF))
            if at == planes - 1:
                rows_out = lax.dynamic_slice(held.pop("out"), (mv.z * plane, 0), (plane, D // 2))
                rows_out = rows_out.astype(F32) + held.pop("out_ring").astype(F32)
                held["out_b"] = rows_out.astype(BF)
            ring = at - (planes - 1) + 1
            if 1 <= ring < planes:
                branch = branch_step(ring, held.pop("branch"))
                if ring < planes - 1:
                    held["branch"] = mv.up(branch.astype(BF))
                else:
                    held["output"] = (hidden_one + branch + bias_down).astype(BF)
            if 0 <= j - 2 < planes:
                sums = lin_items[j - 2].total(held["lin"], held["lin2"], held["lin1"])
                if j - 2 > 0:
                    sums = sums + held.pop("lin_ring").astype(F32)
                if j - 2 < planes - 1:
                    held["lin_ring"] = mv.up(sums.astype(BF))
                else:
                    held["lin_sum"] = sums
            if at == open_out + 2:
                sums = out_item.total(held["out_b"], held["out2"], held["out1"])
                held["out_grad"] = jnp.concatenate(swap_halves(mv, sums), 1)
            if 0 <= f - 2 < 2:
                sums = ffn_items[f - 2].total(
                    held["partials"][f - 2], held["ffn2"], held["ffn1"]
                )
                held[f"unit_grad{f - 2}"] = sums[:units]
            for one, two, new in (("ffn1", "ffn2", got_ffn),):
                if one in held:
                    held[two] = held.pop(one)
                if new is not None:
                    held[one] = new
            if "lin1" in held:
                held["lin2"] = held.pop("lin1")
            if got is not None:
                held["lin1"] = got
            if "out1" in held:
                held["out2"] = held.pop("out1")
            if got_out is not None:
                held["out1"] = got_out
            if at == 0:
                held["down_sum"] = down_sum
                held["attended"] = held["attended"].reshape(seqs, LENGTH, H, HD)
                held["scores"] = scores_back(held["attended"])
                partials = [dot_tn(v, held["norm"], BF) for v in held["grads"]]
                held["partials"] = partials
            if at == 1:
                held["q"], held["kv"] = lin_back(held.pop("scores"), held.pop("attended"))
            if at == 1:
                both = jnp.concatenate([core_half(mv, held["q"]), core_half(mv, held["kv"])], 1)
                held["lin"] = dot_tn(norm_both, both, BF)
            if at == 2:
                grad_norm_one = dot_nt(held.pop("q"), w_query) + dot_nt(held.pop("kv"), w_keyval)
                _, norm_one_back = jax.vjp(rms_scale, x_value, gain_one)
                grad_rms_one, grad_gain_one = norm_one_back(grad_norm_one)
                held["input_grad"] = (grad_hidden + grad_rms_one).astype(BF)
                down_bias_sum = jnp.sum(cotangent, axis=0, dtype=F32)
                part = D // n
                small = jnp.stack([grad_gain_one, grad_gain_two, down_bias_sum])
                small = small.reshape(3, planes, 2, 2, 2, part).transpose(2, 3, 4, 1, 0, 5)
                held["small"] = small
                bias = jnp.stack([jnp.sum(v, axis=0, dtype=F32) for v in held.pop("grads")])
                bias = bias.reshape(2, 2, 2, padded)[..., :units]
                held["bias"] = bias.transpose(1, 2, 0, 3)
            for stage, (coordinate, move) in enumerate(
                ((mv.y, mv.over_y), (mv.x, mv.over_x), (mv.core, mv.other))
            ):
                if at == 3 + stage:
                    for name in ("small", "bias")[: 2 if stage < 2 else 1]:
                        whole = held[name]
                        keep = lax.dynamic_index_in_dim(whole, coordinate, 0, keepdims=False)
                        away = lax.dynamic_index_in_dim(whole, 1 - coordinate, 0, keepdims=False)
                        held[name] = keep + move(away)
            for step in range(1, planes):
                if at == min(6 + (step - 1) // 3, last_round):
                    away = lax.dynamic_index_in_dim(
                        held["small"], (mv.z + step) % planes, 0, keepdims=False
                    )
                    held["small_sum"] = held.get("small_sum", 0.0) + mv.up(away, step)
            if at == last_round - 1:
                held["down_grad"] = held.pop("down_sum")[:units].astype(F32)

        small = held["small_sum"] + lax.dynamic_index_in_dim(
            held["small"], mv.z, 0, keepdims=False
        )
        down_grad, gate_grad, up_grad = (
            held[k] for k in ("down_grad", "unit_grad0", "unit_grad1")
        )
        first, second = swap_halves(mv, held["lin_sum"])
        q_grad = jnp.concatenate([first[:, : D // 2], second[:, : D // 2]], 1)
        kv_grad = jnp.concatenate([first[:, D // 2 :], second[:, D // 2 :]], 1)

        return (
            held["output"],
            held["input_grad"],
            small[0],
            q_grad,
            kv_grad,
            held["out_grad"],
            small[1],
            gate_grad,
            held["bias"][0],
            up_grad,
            held["bias"][1],
            down_grad,
            small[2],
        )

    return body


def solution(mesh):
    matrix, vector = P("dp", None), P("dp")
    return jax.shard_map(
        make_body(mesh.shape["dp"]),
        mesh=mesh,
        in_specs=(
            matrix,
            vector,
            vector,
            matrix,
            matrix,
            matrix,
            vector,
            matrix,
            vector,
            matrix,
            vector,
            matrix,
            vector,
            matrix,
        ),
        out_specs=(
            matrix,
            matrix,
            vector,
            matrix,
            matrix,
            matrix,
            vector,
            matrix,
            vector,
            matrix,
            vector,
            matrix,
            vector,
        ),
        check_vma=False,
    )
```

```python
import functools

import jax
import jax.numpy as jnp
from jax import lax
from jax.experimental import pallas as pl
from jax.experimental.pallas import tpu as pltpu
from jax.experimental.layout import Layout, with_layout_constraint
from jax.sharding import PartitionSpec as P

D = 2560
H = 10
HD = 256
LENGTH = 256
F32 = jnp.float32
BF = jnp.bfloat16
EPS = 1e-06


ROWS = Layout((0, 1))


def row_major(value):
    return with_layout_constraint(value, ROWS)


def rms_scale(values, gain):
    return values * lax.rsqrt(jnp.mean(values * values, axis=-1, keepdims=True) + EPS) * gain


def angles(positions):
    quarter = HD // 4
    ladder = jnp.arange(quarter, dtype=F32)
    freq = 10000.0 ** (-2.0 * ladder / (HD // 2))
    angle = positions.astype(F32)[:, None] * freq[None, :]
    return (jnp.cos(angle), jnp.sin(angle))


def rotate(values, cosine, sine):
    quarter = cosine.shape[-1]
    first = values[..., :quarter]
    second = values[..., quarter : 2 * quarter]
    rest = values[..., 2 * quarter :]
    return jnp.concatenate(
        [first * cosine - second * sine, second * cosine + first * sine, rest], -1
    )


def dot_tn(left, right, out=F32):
    return lax.dot_general(
        left, right, (((0,), (0,)), ((), ())), preferred_element_type=F32
    ).astype(out)


def dot_nt(left, right):
    return lax.dot_general(left, right, (((1,), (1,)), ((), ())), preferred_element_type=F32)


def dot_nn(left, right):
    return jnp.dot(left, right, preferred_element_type=F32)


def glu_tanh(gate, up):
    return jax.nn.gelu(gate, approximate=True) * up


class Moves:
    def __init__(self, n):
        self.n = n
        self.planes = n // 8
        me = lax.axis_index("dp")
        self.core = me % 2
        self.x = (me // 2) % 2
        self.y = (me // 4) % 2
        self.z = me // 8

    def flip(self, value, bit):
        return lax.ppermute(value, "dp", [(i, i ^ bit) for i in range(self.n)])

    def other(self, value):
        return self.flip(value, 1)

    def over_x(self, value):
        return self.flip(value, 2)

    def over_y(self, value):
        return self.flip(value, 4)

    def lines(self):
        return [[z * 8 + at + core for z in range(self.planes) for core in (0, 1)] for at in (0, 2, 4, 6)]

    def squares(self):
        return [
            [z * 8 + at + core for at in (0, 2, 4, 6)]
            for z in range(self.planes)
            for core in (0, 1)
        ]

    def up(self, value, steps=1):
        return lax.ppermute(value, "dp", [(i, (i + 8 * steps) % self.n) for i in range(self.n)])


def fence(values):
    return lax.optimization_barrier(values)


def place_kernel(at_ref, mine, theirs, *refs):
    whole = refs[-1]

    @pl.when(pl.program_id(0) < 4)
    def _():
        whole[...] = mine[...]

    @pl.when(pl.program_id(0) >= 4)
    def _():
        whole[...] = theirs[...]


class Rows:
    def __init__(self, mv, rows, width, dtype):
        self.mv, self.rows = mv, rows
        self.shape = jax.ShapeDtypeStruct((mv.n * rows, width), dtype)
        self.whole = None

    def put(self, step, blocks):
        mv, rows = self.mv, self.rows
        z = (mv.z - step) % mv.planes
        at = [
            ((z * 2 + (mv.y ^ fy)) * 2 + (mv.x ^ fx)) * 2 + (mv.core ^ flip)
            for flip in (0, 1)
            for fy in (0, 1)
            for fx in (0, 1)
        ]
        if rows % 16:
            whole = self.whole
            if whole is None:
                whole = jnp.zeros(self.shape.shape, self.shape.dtype)
            for j in range(8):
                block = blocks[j // 4][(j % 4) * rows : (j % 4 + 1) * rows]
                whole = lax.dynamic_update_slice(whole, block, (at[j] * rows, 0))
            self.whole = whole
            return
        width = self.shape.shape[1]
        before = [] if self.whole is None else [self.whole]
        self.whole = pl.pallas_call(
            place_kernel,
            out_shape=self.shape,
            grid_spec=pltpu.PrefetchScalarGridSpec(
                num_scalar_prefetch=1,
                grid=(8,),
                in_specs=[
                    pl.BlockSpec((rows, width), lambda j, at: (jnp.minimum(j, 3), 0)),
                    pl.BlockSpec((rows, width), lambda j, at: (jnp.maximum(j - 4, 0), 0)),
                ]
                + [pl.BlockSpec(memory_space=pl.ANY)] * len(before),
                out_specs=pl.BlockSpec((rows, width), lambda j, at: (at[j], 0)),
            ),
            input_output_aliases={3: 0} if before else {},
            name="place_rows",
        )(jnp.stack(at).astype(jnp.int32), *blocks, *before)

    def done(self):
        return row_major(self.whole)


def gather_weights(mv, to_all, late, late_round, block, block_rounds, held, work):
    halves = [block[: block.shape[0] // 2], block[block.shape[0] // 2 :]]
    arrived = []
    rows = to_all[0].shape[0]
    half = rows // 2
    builders = [Rows(mv, rows, v.shape[1], v.dtype) for v in to_all]
    items = [(i, k) for i in range(len(to_all)) for k in range(mv.planes)]
    piece = list(to_all)
    first = second = whole = None
    starts = []
    for at in range(len(items) + 3):
        placed = [b.whole for b in builders]
        state = (piece, first, second, whole, halves, placed, held)
        if at <= late_round:
            late, state = fence((late, state))
        else:
            state = fence(state)
        piece, first, second, whole, halves, placed, now = state
        held.update(now)
        for builder, value in zip(builders, placed):
            builder.whole = value
        send_x, send_y = [], []
        new_first = new_second = new_whole = None
        fresh = at < len(items)
        if fresh:
            i, k = items[at]
            send_x.append(piece[i])
            send_y.append(piece[i])
        joined = fresh and first is not None and first[1].shape[1] == piece[i].shape[1]
        if first is not None:
            own, from_x, from_y = first
            diag_b, diag_a = from_y[half:rows], from_x[:half]
            if joined or not fresh:
                send_x.append(diag_b)
                send_y.append(diag_a)
            else:
                diag_b, diag_a = mv.over_x(diag_b), mv.over_y(diag_a)
        if send_x:
            got_x = mv.over_x(jnp.concatenate(send_x, 0))
            got_y = mv.over_y(jnp.concatenate(send_y, 0))
        if first is not None:
            if joined or not fresh:
                start = rows if fresh else 0
                diag_b, diag_a = got_x, got_y
            else:
                start = 0
            new_second = (own, from_x, from_y, diag_a, diag_b)
            starts.append(start)
        if fresh:
            new_first = (piece[i], got_x, got_y)
            if k < mv.planes - 1:
                piece[i] = mv.up(piece[i])
        if second is not None:
            own, from_x, from_y, diag_a, diag_b = second
            start = starts[at - 2]
            block = jnp.concatenate(
                [
                    own,
                    from_x[:rows],
                    from_y[:rows],
                    diag_a[start : start + half],
                    diag_b[start : start + half],
                ],
                0,
            )
            new_whole = (block, mv.other(block))
        if at in block_rounds:
            which = block_rounds.index(at) % 2
            halves[which] = mv.up(halves[which])
            arrived.append(halves[which])
        if whole is not None:
            i, k = items[at - 3]
            builders[i].put(k, whole)
        work(at - mv.planes - 3, placed[0])
        first, second, whole = new_first, new_second, new_whole
    arrived = [jnp.concatenate(arrived[i : i + 2], 0) for i in range(0, len(arrived), 2)]
    return [b.done() for b in builders], late, arrived


def mine_of(mv, value, axis=0):
    size = value.shape[axis] // 2
    return lax.dynamic_slice_in_dim(value, mv.core * size, size, axis)


def theirs_of(mv, value, axis=0):
    size = value.shape[axis] // 2
    return lax.dynamic_slice_in_dim(value, (1 - mv.core) * size, size, axis)


def swap_halves(mv, total):
    rows = total.shape[0] // 2
    mine = lax.dynamic_slice(total, (mv.core * rows, 0), (rows, total.shape[1]))
    theirs = mv.other(lax.dynamic_slice(total, ((1 - mv.core) * rows, 0), (rows, total.shape[1])))
    return jnp.where(mv.core == 0, mine, theirs), jnp.where(mv.core == 0, theirs, mine)


def core_half(mv, value):
    width = value.shape[1] // 2
    mine = jnp.where(mv.core == 0, value[:, :width], value[:, width:])
    theirs = jnp.where(mv.core == 0, value[:, width:], value[:, :width])
    return jnp.concatenate([mine, mv.other(theirs)], 0)


def make_body(n):
    def body(
        tokens,
        doc_positions,
        attn_gain,
        q_weight,
        kv_weight,
        out_weight,
        ffn_gain,
        gate_weight,
        gate_bias,
        up_weight,
        up_bias,
        down_weight,
        down_bias,
        cotangent,
    ):
        mv = Moves(n)
        head_scale = HD ** (-0.5)
        rows = tokens.shape[0]
        seqs = rows // LENGTH
        small = jnp.stack([attn_gain, ffn_gain, down_bias], 1)
        small = jnp.pad(small, ((0, 0), (0, 125)))
        units = gate_weight.shape[0]
        padded = -(-(units + 2) // 128) * 128

        def pad_rows(value):
            return jnp.pad(value, ((0, padded - units), (0, 0)))

        bias_rows = jnp.pad(
            jnp.stack([gate_bias, up_bias]), ((0, padded - units - 2), (0, D - units))
        )
        ffn = jnp.concatenate(
            [pad_rows(down_weight), gate_weight, bias_rows, pad_rows(up_weight)], 0
        )
        rounds = 2 * mv.planes
        x_value = tokens.astype(F32)
        cosine, sine = angles(doc_positions)
        index = jnp.arange(LENGTH)
        distance = index[:, None] - index[None, :]
        allowed = (distance[None] >= 0) & (
            distance[None] <= doc_positions.reshape(seqs, LENGTH)[:, :, None]
        )
        held = {}

        def split_qkv(w_qkv):
            small = w_qkv[:, D + 2 * HD :].T.astype(F32)
            return w_qkv[:, :D], w_qkv[:, D : D + 2 * HD], small

        def attention(at, w_qkv):
            if at == 1:
                w_query, w_keyval, small = split_qkv(w_qkv)
                norm_one_b = rms_scale(x_value, small[0]).astype(BF)
                held["norm_one"] = norm_one_b
                q_lin = dot_nn(norm_one_b, w_query).reshape(rows, H, HD)
                query = rotate(q_lin, cosine[:, None, :], sine[:, None, :]) * head_scale
                held["query"] = query.astype(BF).reshape(seqs, LENGTH, H, HD)
                held["kv"] = dot_nn(norm_one_b, w_keyval)
            if at == 2:
                kv_lin = held.pop("kv")
                key = rotate(kv_lin[:, :HD], cosine, sine).astype(BF)
                held["key"] = key.reshape(seqs, LENGTH, HD)
                held["value"] = kv_lin[:, HD:].astype(BF).reshape(seqs, LENGTH, HD)
                logits = jnp.einsum(
                    "sqhd,skd->shqk", held["query"], held["key"], preferred_element_type=F32
                )
                held["logits"] = jnp.where(allowed[:, None], logits, -1e30)
            if at == 3:
                logits = held.pop("logits")
                weights = jnp.exp(logits - jnp.max(logits, axis=-1, keepdims=True))
                held["soft"] = weights / jnp.sum(weights, axis=-1, keepdims=True)
                held["probs"] = held["soft"].astype(BF)
                held["attended"] = (
                    jnp.einsum(
                        "shqk,skd->sqhd",
                        held["probs"],
                        held["value"],
                        preferred_element_type=F32,
                    )
                    .reshape(rows, H * HD)
                    .astype(BF)
                )

        (w_qkv, w_out), ffn, cots = gather_weights(
            mv,
            [jnp.concatenate([q_weight, kv_weight, small], 1), out_weight],
            ffn,
            rounds - 1,
            cotangent,
            [mv.planes - 1, *range(rounds - 2, rounds + 3)],
            held,
            attention,
        )
        cots = [cotangent, *cots]
        w_query, w_keyval, small = split_qkv(w_qkv)
        gain_one, gain_two, bias_down = small[0], small[1], small[2]
        norm_one_b, query, key, value = (held[k] for k in ("norm_one", "query", "key", "value"))
        soft, probs, attended = (held[k] for k in ("soft", "probs", "attended"))
        ffn = lax.all_gather(ffn, "dp", axis=0, tiled=True, axis_index_groups=mv.squares())
        hidden_one = x_value + dot_nn(attended, w_out)
        norm_two_b = rms_scale(hidden_one, gain_two).astype(BF)

        order = [*range(1, mv.planes), 0]
        norms, cots, norm_pieces, cot_pieces = [norm_two_b], list(cots), [], []
        swap_early = [attended, norm_one_b]
        swapped = []

        def piece_work(step):
            gate = dot_nt(norm_pieces[step], w_gate) + b_gate
            up = dot_nt(norm_pieces[step], w_up) + b_up
            grad_act = dot_nt(cot_pieces[step], w_down)
            act, act_back = jax.vjp(glu_tanh, gate, up)
            grad_gate, grad_up = (v.astype(BF) for v in act_back(grad_act))
            partial = dot_nn(grad_gate, w_gate) + dot_nn(grad_up, w_up)
            return act.astype(BF), grad_gate, grad_up, partial[:rows], partial[rows:].astype(BF)

        acts, grads_all = [], ([], [])
        sends, received, parts, gots, partials = {}, None, {}, {}, None
        last = mv.planes + 1
        for at in range(last + 1):
            norms, cots, swap_early, norm_pieces, cot_pieces, acts, grads_all = fence(
                (norms, cots, swap_early, norm_pieces, cot_pieces, acts, grads_all)
            )
            if at == last:
                sends, norm_pieces, acts, grads_all = fence((sends, norm_pieces, acts, grads_all))
            if at == 1:
                ffn = ffn.reshape(4, 3 * padded, D)
                w_down, w_gate, w_up = (
                    ffn[:, i * padded : (i + 1) * padded].reshape(4 * padded, D) for i in range(3)
                )
                b_gate, b_up = (
                    ffn[:, padded + units + i, :padded].reshape(4 * padded).astype(F32)
                    for i in range(2)
                )
                w_down, w_gate, w_up, b_gate, b_up, norm_pieces = fence(
                    (w_down, w_gate, w_up, b_gate, b_up, norm_pieces)
                )
            if at <= mv.planes - 2:
                norms.append(mv.up(norms[at]))
            if 4 + at < mv.planes:
                cots.append(mv.up(cots[3 + at]))
            if at - 2 in sends:
                received = mv.up(sends.pop(at - 2))
            if at < mv.planes:
                norm_pieces.append(jnp.concatenate([norms[at], mv.other(norms[at])], 0))
                cot_pieces.append(jnp.concatenate([cots[at], mv.other(cots[at])], 0))
            if at in (0, mv.planes):
                early = swap_early[min(at, 1)]
                swapped.append(jnp.concatenate([early, mv.other(early)], 0))
            step = at - 1
            if 0 <= step < mv.planes:
                act, grad_gate, grad_up, own_part, their_part = piece_work(step)
                acts.append(act)
                grads_all[0].append(grad_gate)
                grads_all[1].append(grad_up)
                parts[step] = own_part
                gots[step] = mv.other(their_part)
            if at == last:
                acts = jnp.concatenate(acts, 0)
                grads_all = [jnp.concatenate(v, 0) for v in grads_all]
                cot_all = jnp.concatenate(cot_pieces, 0)
                norm_all = jnp.concatenate(norm_pieces, 0)
                acts_two = acts.reshape(mv.planes, 2, rows, 4 * padded)
                branch_mine, branch_other = (
                    dot_nn(acts_two[:, i].reshape(mv.planes * rows, 4 * padded), w_down)
                    .astype(BF)
                    .reshape(mv.planes, rows, D)
                    for i in (0, 1)
                )
                partials = (branch_mine, mv.other(branch_other), dot_tn(acts, cot_all, BF))
            (
                norms,
                cots,
                norm_pieces,
                cot_pieces,
                swapped,
                acts,
                grads_all,
                parts,
                gots,
                received,
                partials,
            ) = (
                fence(
                    (
                        norms,
                        cots,
                        norm_pieces,
                        cot_pieces,
                        swapped,
                        acts,
                        grads_all,
                        parts,
                        gots,
                        received,
                        partials,
                    )
                )
            )
            if step >= 1:
                done = step if step < mv.planes else 0
                total = parts.pop(done) + gots.pop(done).astype(F32)
                if received is not None:
                    total = total + received.astype(F32)
                    received = None
                if done:
                    sends[done] = total.astype(BF)
        grad_norm_two = total
        attended_both, norm_both = swapped
        branch_mine, branch_got, down_partial = partials

        def branch_step(ring, received):
            at_piece = order[ring]
            branch = branch_mine[at_piece].astype(F32) + branch_got[at_piece].astype(F32)
            return branch if received is None else branch + received.astype(F32)

        def ffn_sum(value):
            return lax.psum_scatter(
                value, "dp", scatter_dimension=0, tiled=True, axis_index_groups=mv.squares()
            )

        down_sum = ffn_sum(down_partial)
        branch_sent = branch_step(0, None).astype(BF)
        grad_norm_two, branch_sent = fence((grad_norm_two, branch_sent))
        branch_ring = mv.up(branch_sent)

        _, norm_two_back = jax.vjp(rms_scale, hidden_one, gain_two)
        grad_rms_two, grad_gain_two = norm_two_back(grad_norm_two)
        grad_hidden = cotangent.astype(F32) + grad_rms_two
        grad_hidden_b = grad_hidden.astype(BF)

        out_partial = dot_tn(attended_both, core_half(mv, grad_hidden_b), BF)
        grad_attended = dot_nt(grad_hidden_b, w_out).astype(BF)
        out_partial, grad_attended, grads_all, norm_all, branch_ring = fence(
            (out_partial, grad_attended, grads_all, norm_all, branch_ring)
        )
        held = {"attended": grad_attended, "grads": grads_all, "norm": norm_all, "out": out_partial, "branch": branch_ring}

        def scores_back(grad_attended):
            grad_probs = jnp.einsum(
                "sqhd,skd->shqk", grad_attended, value, preferred_element_type=F32
            )
            return (
                soft * (grad_probs - jnp.sum(grad_probs * soft, axis=-1, keepdims=True))
            ).astype(BF)

        def lin_back(grad_scores, grad_attended):
            grad_value = jnp.einsum(
                "shqk,sqhd->skd", probs, grad_attended, preferred_element_type=F32
            ).reshape(rows, HD)
            grad_query = jnp.einsum(
                "shqk,skd->sqhd", grad_scores, key, preferred_element_type=F32
            ).reshape(rows, H, HD)
            grad_key = jnp.einsum(
                "shqk,sqhd->skd", grad_scores, query, preferred_element_type=F32
            ).reshape(rows, HD)
            grad_kv_lin = jnp.concatenate(
                [rotate(grad_key, cosine, -sine), grad_value], 1
            ).astype(BF)
            grad_q_lin = (
                rotate(grad_query * head_scale, cosine[:, None, :], -sine[:, None, :])
                .reshape(rows, H * HD)
                .astype(BF)
            )
            return grad_q_lin, grad_kv_lin

        chip = D // (n // 2)
        plane = 4 * chip

        class Scatter:
            def __init__(self, base, chip):
                self.base, self.chip, self.half, self.at = base, chip, chip // 2, 0

            def block(self, array, flip_y, flip_x, low=True, high=True):
                index = (mv.y ^ flip_y) * 2 + (mv.x ^ flip_x)
                start = self.base + index * self.chip + (0 if low else self.half)
                count = self.half * (low + high)
                return lax.dynamic_slice(array, (start, 0), (count, array.shape[1]))

            def open(self, array, send_x, send_y):
                send_x += [
                    self.block(array, 1, 1, high=False),
                    self.block(array, 0, 1, high=False),
                ]
                send_y += [
                    self.block(array, 1, 1, low=False),
                    self.block(array, 1, 0, low=False),
                ]

            def close(self, array, got, send_x, send_y):
                from_x, from_y = got
                self.at = sum(v.shape[0] for v in send_x)
                last_x = self.block(array, 0, 1, low=False).astype(F32)
                last_y = self.block(array, 1, 0, high=False).astype(F32)
                send_x.append((last_x + from_y[: self.half].astype(F32)).astype(BF))
                send_y.append((last_y + from_x[: self.half].astype(F32)).astype(BF))

            def total(self, array, got, more):
                (from_x, from_y), (more_x, more_y) = got, more
                last = slice(self.at, self.at + self.half)
                kept = slice(self.half, self.chip)
                sums = self.block(array, 0, 0).astype(F32)
                sums += jnp.concatenate([from_x[kept], more_x[last]], 0).astype(F32)
                sums += jnp.concatenate([more_y[last], from_y[kept]], 0).astype(F32)
                return sums

        def exchange(send_x, send_y):
            if not send_x:
                return None
            send_x, send_y, now = fence(
                (jnp.concatenate(send_x, 0), jnp.concatenate(send_y, 0), held)
            )
            held.update(now)
            return mv.over_x(send_x), mv.over_y(send_y)

        planes = mv.planes
        lin_items = [Scatter(((mv.z - k) % planes) * plane, chip) for k in [*range(1, planes), 0]]
        out_item = Scatter(0, chip)
        ffn_items = [Scatter(0, padded), Scatter(0, padded)]
        open_lin, open_out = 2, max(4, planes)
        last_round = max(open_lin + planes + 1, open_out + 2, 6 + (planes - 2) // 3, 2 * planes - 3)
        for at in range(last_round + 1):
            now = fence(held)
            held.update(now)
            send_x, send_y = [], []
            j = at - open_lin
            if 0 <= j < planes:
                lin_items[j].open(held["lin"], send_x, send_y)
            if 0 <= j - 1 < planes:
                lin_items[j - 1].close(held["lin"], held["lin1"], send_x, send_y)
            out_x, out_y = [], []
            if at == open_out:
                out_item.open(held["out_b"], out_x, out_y)
            if at == open_out + 1:
                out_item.close(held["out_b"], held["out1"], out_x, out_y)
            ffn_x, ffn_y = [], []
            f = at - 1
            if 0 <= f < 2:
                ffn_items[f].open(held["partials"][f], ffn_x, ffn_y)
            if 0 <= f - 1 < 2:
                ffn_items[f - 1].close(held["partials"][f - 1], held["ffn1"], ffn_x, ffn_y)
            got, got_out = exchange(send_x, send_y), exchange(out_x, out_y)
            got_ffn = exchange(ffn_x, ffn_y)
            if at < planes - 1:
                z = (mv.z - at - 1) % planes
                rows_out = lax.dynamic_slice(held["out"], (z * plane, 0), (plane, D // 2))
                if at > 0:
                    rows_out = rows_out.astype(F32) + held.pop("out_ring").astype(F32)
                held["out_ring"] = mv.up(rows_out.astype(BF))
            if at == planes - 1:
                rows_out = lax.dynamic_slice(held.pop("out"), (mv.z * plane, 0), (plane, D // 2))
                rows_out = rows_out.astype(F32) + held.pop("out_ring").astype(F32)
                held["out_b"] = rows_out.astype(BF)
            ring = at - (planes - 1) + 1
            if 1 <= ring < planes:
                branch = branch_step(ring, held.pop("branch"))
                if ring < planes - 1:
                    held["branch"] = mv.up(branch.astype(BF))
                else:
                    held["output"] = (hidden_one + branch + bias_down).astype(BF)
            if 0 <= j - 2 < planes:
                sums = lin_items[j - 2].total(held["lin"], held["lin2"], held["lin1"])
                if j - 2 > 0:
                    sums = sums + held.pop("lin_ring").astype(F32)
                if j - 2 < planes - 1:
                    held["lin_ring"] = mv.up(sums.astype(BF))
                else:
                    held["lin_sum"] = sums
            if at == open_out + 2:
                sums = out_item.total(held["out_b"], held["out2"], held["out1"])
                held["out_grad"] = jnp.concatenate(swap_halves(mv, sums), 1)
            if 0 <= f - 2 < 2:
                sums = ffn_items[f - 2].total(
                    held["partials"][f - 2], held["ffn2"], held["ffn1"]
                )
                held[f"unit_grad{f - 2}"] = sums[:units]
            for one, two, new in (("ffn1", "ffn2", got_ffn),):
                if one in held:
                    held[two] = held.pop(one)
                if new is not None:
                    held[one] = new
            if "lin1" in held:
                held["lin2"] = held.pop("lin1")
            if got is not None:
                held["lin1"] = got
            if "out1" in held:
                held["out2"] = held.pop("out1")
            if got_out is not None:
                held["out1"] = got_out
            if at == 0:
                held["down_sum"] = down_sum
                held["attended"] = held["attended"].reshape(seqs, LENGTH, H, HD)
                held["scores"] = scores_back(held["attended"])
                partials = [dot_tn(v, held["norm"], BF) for v in held["grads"]]
                held["partials"] = partials
            if at == 1:
                held["q"], held["kv"] = lin_back(held.pop("scores"), held.pop("attended"))
            if at == 1:
                both = jnp.concatenate([core_half(mv, held["q"]), core_half(mv, held["kv"])], 1)
                held["lin"] = dot_tn(norm_both, both, BF)
            if at == 2:
                grad_norm_one = dot_nt(held.pop("q"), w_query) + dot_nt(held.pop("kv"), w_keyval)
                _, norm_one_back = jax.vjp(rms_scale, x_value, gain_one)
                grad_rms_one, grad_gain_one = norm_one_back(grad_norm_one)
                held["input_grad"] = (grad_hidden + grad_rms_one).astype(BF)
                down_bias_sum = jnp.sum(cotangent, axis=0, dtype=F32)
                part = D // n
                small = jnp.stack([grad_gain_one, grad_gain_two, down_bias_sum])
                small = small.reshape(3, planes, 2, 2, 2, part).transpose(2, 3, 4, 1, 0, 5)
                held["small"] = small
                bias = jnp.stack([jnp.sum(v, axis=0, dtype=F32) for v in held.pop("grads")])
                bias = bias.reshape(2, 2, 2, padded)[..., :units]
                held["bias"] = bias.transpose(1, 2, 0, 3)
            for stage, (coordinate, move) in enumerate(
                ((mv.y, mv.over_y), (mv.x, mv.over_x), (mv.core, mv.other))
            ):
                if at == 3 + stage:
                    for name in ("small", "bias")[: 2 if stage < 2 else 1]:
                        whole = held[name]
                        keep = lax.dynamic_index_in_dim(whole, coordinate, 0, keepdims=False)
                        away = lax.dynamic_index_in_dim(whole, 1 - coordinate, 0, keepdims=False)
                        held[name] = keep + move(away)
            for step in range(1, planes):
                if at == min(6 + (step - 1) // 3, last_round):
                    away = lax.dynamic_index_in_dim(
                        held["small"], (mv.z + step) % planes, 0, keepdims=False
                    )
                    held["small_sum"] = held.get("small_sum", 0.0) + mv.up(away, step)
            if at == last_round - 1:
                held["down_grad"] = held.pop("down_sum")[:units].astype(F32)

        small = held["small_sum"] + lax.dynamic_index_in_dim(
            held["small"], mv.z, 0, keepdims=False
        )
        down_grad, gate_grad, up_grad = (
            held[k] for k in ("down_grad", "unit_grad0", "unit_grad1")
        )
        first, second = swap_halves(mv, held["lin_sum"])
        q_grad = jnp.concatenate([first[:, : D // 2], second[:, : D // 2]], 1)
        kv_grad = jnp.concatenate([first[:, D // 2 :], second[:, D // 2 :]], 1)

        return (
            held["output"],
            held["input_grad"],
            small[0],
            q_grad,
            kv_grad,
            held["out_grad"],
            small[1],
            gate_grad,
            held["bias"][0],
            up_grad,
            held["bias"][1],
            down_grad,
            small[2],
        )

    return body


def solution(mesh):
    matrix, vector = P("dp", None), P("dp")
    return jax.shard_map(
        make_body(mesh.shape["dp"]),
        mesh=mesh,
        in_specs=(
            matrix,
            vector,
            vector,
            matrix,
            matrix,
            matrix,
            vector,
            matrix,
            vector,
            matrix,
            vector,
            matrix,
            vector,
            matrix,
        ),
        out_specs=(
            matrix,
            matrix,
            vector,
            matrix,
            matrix,
            matrix,
            vector,
            matrix,
            vector,
            matrix,
            vector,
            matrix,
            vector,
        ),
        check_vma=False,
    )
```

```python
import functools

import jax
import jax.numpy as jnp
from jax import lax
from jax.experimental import pallas as pl
from jax.experimental.pallas import tpu as pltpu
from jax.experimental.layout import Layout, with_layout_constraint
from jax.sharding import PartitionSpec as P

D = 2560
H = 10
HD = 256
LENGTH = 256
F32 = jnp.float32
BF = jnp.bfloat16
EPS = 1e-06


ROWS = Layout((0, 1))


def row_major(value):
    return with_layout_constraint(value, ROWS)


def rms_scale(values, gain):
    return values * lax.rsqrt(jnp.mean(values * values, axis=-1, keepdims=True) + EPS) * gain


def angles(positions):
    quarter = HD // 4
    ladder = jnp.arange(quarter, dtype=F32)
    freq = 10000.0 ** (-2.0 * ladder / (HD // 2))
    angle = positions.astype(F32)[:, None] * freq[None, :]
    return (jnp.cos(angle), jnp.sin(angle))


def rotate(values, cosine, sine):
    quarter = cosine.shape[-1]
    first = values[..., :quarter]
    second = values[..., quarter : 2 * quarter]
    rest = values[..., 2 * quarter :]
    return jnp.concatenate(
        [first * cosine - second * sine, second * cosine + first * sine, rest], -1
    )


def dot_tn(left, right, out=F32):
    return lax.dot_general(
        left, right, (((0,), (0,)), ((), ())), preferred_element_type=F32
    ).astype(out)


def dot_nt(left, right):
    return lax.dot_general(left, right, (((1,), (1,)), ((), ())), preferred_element_type=F32)


def dot_nn(left, right):
    return jnp.dot(left, right, preferred_element_type=F32)


def glu_tanh(gate, up):
    return jax.nn.gelu(gate, approximate=True) * up


class Moves:
    def __init__(self, n):
        self.n = n
        self.planes = n // 8
        me = lax.axis_index("dp")
        self.core = me % 2
        self.x = (me // 2) % 2
        self.y = (me // 4) % 2
        self.z = me // 8

    def flip(self, value, bit):
        return lax.ppermute(value, "dp", [(i, i ^ bit) for i in range(self.n)])

    def other(self, value):
        return self.flip(value, 1)

    def over_x(self, value):
        return self.flip(value, 2)

    def over_y(self, value):
        return self.flip(value, 4)

    def lines(self):
        return [[z * 8 + at + core for z in range(self.planes) for core in (0, 1)] for at in (0, 2, 4, 6)]

    def squares(self):
        return [
            [z * 8 + at + core for at in (0, 2, 4, 6)]
            for z in range(self.planes)
            for core in (0, 1)
        ]

    def up(self, value, steps=1):
        return lax.ppermute(value, "dp", [(i, (i + 8 * steps) % self.n) for i in range(self.n)])


def fence(values):
    return lax.optimization_barrier(values)


def place_kernel(at_ref, mine, theirs, *refs):
    whole = refs[-1]

    @pl.when(pl.program_id(0) < 4)
    def _():
        whole[...] = mine[...]

    @pl.when(pl.program_id(0) >= 4)
    def _():
        whole[...] = theirs[...]


class Rows:
    def __init__(self, mv, rows, width, dtype):
        self.mv, self.rows = mv, rows
        self.shape = jax.ShapeDtypeStruct((mv.n * rows, width), dtype)
        self.whole = None

    def put(self, step, blocks):
        mv, rows = self.mv, self.rows
        z = (mv.z - step) % mv.planes
        at = [
            ((z * 2 + (mv.y ^ fy)) * 2 + (mv.x ^ fx)) * 2 + (mv.core ^ flip)
            for flip in (0, 1)
            for fy in (0, 1)
            for fx in (0, 1)
        ]
        if rows % 16:
            whole = self.whole
            if whole is None:
                whole = jnp.zeros(self.shape.shape, self.shape.dtype)
            for j in range(8):
                block = blocks[j // 4][(j % 4) * rows : (j % 4 + 1) * rows]
                whole = lax.dynamic_update_slice(whole, block, (at[j] * rows, 0))
            self.whole = whole
            return
        width = self.shape.shape[1]
        before = [] if self.whole is None else [self.whole]
        self.whole = pl.pallas_call(
            place_kernel,
            out_shape=self.shape,
            grid_spec=pltpu.PrefetchScalarGridSpec(
                num_scalar_prefetch=1,
                grid=(8,),
                in_specs=[
                    pl.BlockSpec((rows, width), lambda j, at: (jnp.minimum(j, 3), 0)),
                    pl.BlockSpec((rows, width), lambda j, at: (jnp.maximum(j - 4, 0), 0)),
                ]
                + [pl.BlockSpec(memory_space=pl.ANY)] * len(before),
                out_specs=pl.BlockSpec((rows, width), lambda j, at: (at[j], 0)),
            ),
            input_output_aliases={3: 0} if before else {},
            name="place_rows",
        )(jnp.stack(at).astype(jnp.int32), *blocks, *before)

    def done(self):
        return row_major(self.whole)


def gather_weights(mv, to_all, late, late_round, block, block_rounds, held, work):
    halves = [block[: block.shape[0] // 2], block[block.shape[0] // 2 :]]
    arrived = []
    rows = to_all[0].shape[0]
    half = rows // 2
    builders = [Rows(mv, rows, v.shape[1], v.dtype) for v in to_all]
    items = [(i, k) for i in range(len(to_all)) for k in range(mv.planes)]
    piece = list(to_all)
    first = second = whole = None
    starts = []
    for at in range(len(items) + 3):
        placed = [b.whole for b in builders]
        state = (piece, first, second, whole, halves, placed, held)
        if at <= late_round:
            late, state = fence((late, state))
        else:
            state = fence(state)
        piece, first, second, whole, halves, placed, now = state
        held.update(now)
        for builder, value in zip(builders, placed):
            builder.whole = value
        send_x, send_y = [], []
        new_first = new_second = new_whole = None
        fresh = at < len(items)
        if fresh:
            i, k = items[at]
            send_x.append(piece[i])
            send_y.append(piece[i])
        joined = fresh and first is not None and first[1].shape[1] == piece[i].shape[1]
        if first is not None:
            own, from_x, from_y = first
            diag_b, diag_a = from_y[half:rows], from_x[:half]
            if joined or not fresh:
                send_x.append(diag_b)
                send_y.append(diag_a)
            else:
                diag_b, diag_a = mv.over_x(diag_b), mv.over_y(diag_a)
        if send_x:
            got_x = mv.over_x(jnp.concatenate(send_x, 0))
            got_y = mv.over_y(jnp.concatenate(send_y, 0))
        if first is not None:
            if joined or not fresh:
                start = rows if fresh else 0
                diag_b, diag_a = got_x, got_y
            else:
                start = 0
            new_second = (own, from_x, from_y, diag_a, diag_b)
            starts.append(start)
        if fresh:
            new_first = (piece[i], got_x, got_y)
            if k < mv.planes - 1:
                piece[i] = mv.up(piece[i])
        if second is not None:
            own, from_x, from_y, diag_a, diag_b = second
            start = starts[at - 2]
            block = jnp.concatenate(
                [
                    own,
                    from_x[:rows],
                    from_y[:rows],
                    diag_a[start : start + half],
                    diag_b[start : start + half],
                ],
                0,
            )
            new_whole = (block, mv.other(block))
        if at in block_rounds:
            which = block_rounds.index(at) % 2
            halves[which] = mv.up(halves[which])
            arrived.append(halves[which])
        if whole is not None:
            i, k = items[at - 3]
            builders[i].put(k, whole)
        work(at - mv.planes - 3, placed[0])
        first, second, whole = new_first, new_second, new_whole
    arrived = [jnp.concatenate(arrived[i : i + 2], 0) for i in range(0, len(arrived), 2)]
    return [b.done() for b in builders], late, arrived


def mine_of(mv, value, axis=0):
    size = value.shape[axis] // 2
    return lax.dynamic_slice_in_dim(value, mv.core * size, size, axis)


def theirs_of(mv, value, axis=0):
    size = value.shape[axis] // 2
    return lax.dynamic_slice_in_dim(value, (1 - mv.core) * size, size, axis)


def swap_halves(mv, total):
    rows = total.shape[0] // 2
    mine = lax.dynamic_slice(total, (mv.core * rows, 0), (rows, total.shape[1]))
    theirs = mv.other(lax.dynamic_slice(total, ((1 - mv.core) * rows, 0), (rows, total.shape[1])))
    return jnp.where(mv.core == 0, mine, theirs), jnp.where(mv.core == 0, theirs, mine)


def core_half(mv, value):
    width = value.shape[1] // 2
    mine = jnp.where(mv.core == 0, value[:, :width], value[:, width:])
    theirs = jnp.where(mv.core == 0, value[:, width:], value[:, :width])
    return jnp.concatenate([mine, mv.other(theirs)], 0)


def make_body(n):
    def body(
        tokens,
        doc_positions,
        attn_gain,
        q_weight,
        kv_weight,
        out_weight,
        ffn_gain,
        gate_weight,
        gate_bias,
        up_weight,
        up_bias,
        down_weight,
        down_bias,
        cotangent,
    ):
        mv = Moves(n)
        head_scale = HD ** (-0.5)
        rows = tokens.shape[0]
        seqs = rows // LENGTH
        small = jnp.stack([attn_gain, ffn_gain, down_bias], 1)
        small = jnp.pad(small, ((0, 0), (0, 125)))
        units = gate_weight.shape[0]
        padded = -(-(units + 2) // 128) * 128

        def pad_rows(value):
            return jnp.pad(value, ((0, padded - units), (0, 0)))

        bias_rows = jnp.pad(
            jnp.stack([gate_bias, up_bias]), ((0, padded - units - 2), (0, D - units))
        )
        ffn = jnp.concatenate(
            [pad_rows(down_weight), gate_weight, bias_rows, pad_rows(up_weight)], 0
        )
        rounds = 2 * mv.planes
        x_value = tokens.astype(F32)
        cosine, sine = angles(doc_positions)
        index = jnp.arange(LENGTH)
        distance = index[:, None] - index[None, :]
        allowed = (distance[None] >= 0) & (
            distance[None] <= doc_positions.reshape(seqs, LENGTH)[:, :, None]
        )
        held = {}

        def split_qkv(w_qkv):
            small = w_qkv[:, D + 2 * HD :].T.astype(F32)
            return w_qkv[:, :D], w_qkv[:, D : D + 2 * HD], small

        def attention(at, w_qkv):
            if at == 1:
                w_query, w_keyval, small = split_qkv(w_qkv)
                norm_one_b = rms_scale(x_value, small[0]).astype(BF)
                held["norm_one"] = norm_one_b
                q_lin = dot_nn(norm_one_b, w_query).reshape(rows, H, HD)
                query = rotate(q_lin, cosine[:, None, :], sine[:, None, :]) * head_scale
                held["query"] = query.astype(BF).reshape(seqs, LENGTH, H, HD)
                held["kv"] = dot_nn(norm_one_b, w_keyval)
            if at == 2:
                kv_lin = held.pop("kv")
                key = rotate(kv_lin[:, :HD], cosine, sine).astype(BF)
                held["key"] = key.reshape(seqs, LENGTH, HD)
                held["value"] = kv_lin[:, HD:].astype(BF).reshape(seqs, LENGTH, HD)
                logits = jnp.einsum(
                    "sqhd,skd->shqk", held["query"], held["key"], preferred_element_type=F32
                )
                held["logits"] = jnp.where(allowed[:, None], logits, -1e30)
            if at == 3:
                logits = held.pop("logits")
                weights = jnp.exp(logits - jnp.max(logits, axis=-1, keepdims=True))
                held["soft"] = weights / jnp.sum(weights, axis=-1, keepdims=True)
                held["probs"] = held["soft"].astype(BF)
                held["attended"] = (
                    jnp.einsum(
                        "shqk,skd->sqhd",
                        held["probs"],
                        held["value"],
                        preferred_element_type=F32,
                    )
                    .reshape(rows, H * HD)
                    .astype(BF)
                )

        (w_qkv, w_out), ffn, cots = gather_weights(
            mv,
            [jnp.concatenate([q_weight, kv_weight, small], 1), out_weight],
            ffn,
            rounds,
            cotangent,
            [mv.planes - 1, *range(rounds - 2, rounds + 3)],
            held,
            attention,
        )
        cots = [cotangent, *cots]
        w_query, w_keyval, small = split_qkv(w_qkv)
        gain_one, gain_two, bias_down = small[0], small[1], small[2]
        norm_one_b, query, key, value = (held[k] for k in ("norm_one", "query", "key", "value"))
        soft, probs, attended = (held[k] for k in ("soft", "probs", "attended"))
        ffn = lax.all_gather(ffn, "dp", axis=0, tiled=True, axis_index_groups=mv.squares())
        hidden_one = x_value + dot_nn(attended, w_out)
        norm_two_b = rms_scale(hidden_one, gain_two).astype(BF)

        order = [*range(1, mv.planes), 0]
        norms, cots, norm_pieces, cot_pieces = [norm_two_b], list(cots), [], []
        swap_early = [attended, norm_one_b]
        swapped = []

        def piece_work(step):
            gate = dot_nt(norm_pieces[step], w_gate) + b_gate
            up = dot_nt(norm_pieces[step], w_up) + b_up
            grad_act = dot_nt(cot_pieces[step], w_down)
            act, act_back = jax.vjp(glu_tanh, gate, up)
            grad_gate, grad_up = (v.astype(BF) for v in act_back(grad_act))
            partial = dot_nn(grad_gate, w_gate) + dot_nn(grad_up, w_up)
            return act.astype(BF), grad_gate, grad_up, partial[:rows], partial[rows:].astype(BF)

        acts, grads_all = [], ([], [])
        sends, received, parts, gots, partials = {}, None, {}, {}, None
        last = mv.planes + 1
        for at in range(last + 1):
            norms, cots, swap_early, norm_pieces, cot_pieces, acts, grads_all = fence(
                (norms, cots, swap_early, norm_pieces, cot_pieces, acts, grads_all)
            )
            if at == last:
                sends, norm_pieces, acts, grads_all = fence((sends, norm_pieces, acts, grads_all))
            if at == 1:
                ffn = ffn.reshape(4, 3 * padded, D)
                w_down, w_gate, w_up = (
                    ffn[:, i * padded : (i + 1) * padded].reshape(4 * padded, D) for i in range(3)
                )
                b_gate, b_up = (
                    ffn[:, padded + units + i, :padded].reshape(4 * padded).astype(F32)
                    for i in range(2)
                )
                w_down, w_gate, w_up, b_gate, b_up, norm_pieces = fence(
                    (w_down, w_gate, w_up, b_gate, b_up, norm_pieces)
                )
            if at <= mv.planes - 2:
                norms.append(mv.up(norms[at]))
            if 4 + at < mv.planes:
                cots.append(mv.up(cots[3 + at]))
            if at - 2 in sends:
                received = mv.up(sends.pop(at - 2))
            if at < mv.planes:
                norm_pieces.append(jnp.concatenate([norms[at], mv.other(norms[at])], 0))
                cot_pieces.append(jnp.concatenate([cots[at], mv.other(cots[at])], 0))
            if at in (0, mv.planes):
                early = swap_early[min(at, 1)]
                swapped.append(jnp.concatenate([early, mv.other(early)], 0))
            step = at - 1
            if 0 <= step < mv.planes:
                act, grad_gate, grad_up, own_part, their_part = piece_work(step)
                acts.append(act)
                grads_all[0].append(grad_gate)
                grads_all[1].append(grad_up)
                parts[step] = own_part
                gots[step] = mv.other(their_part)
            if at == last:
                acts = jnp.concatenate(acts, 0)
                grads_all = [jnp.concatenate(v, 0) for v in grads_all]
                cot_all = jnp.concatenate(cot_pieces, 0)
                norm_all = jnp.concatenate(norm_pieces, 0)
                acts_two = acts.reshape(mv.planes, 2, rows, 4 * padded)
                branch_mine, branch_other = (
                    dot_nn(acts_two[:, i].reshape(mv.planes * rows, 4 * padded), w_down)
                    .astype(BF)
                    .reshape(mv.planes, rows, D)
                    for i in (0, 1)
                )
                partials = (branch_mine, mv.other(branch_other), dot_tn(acts, cot_all, BF))
            (
                norms,
                cots,
                norm_pieces,
                cot_pieces,
                swapped,
                acts,
                grads_all,
                parts,
                gots,
                received,
                partials,
            ) = (
                fence(
                    (
                        norms,
                        cots,
                        norm_pieces,
                        cot_pieces,
                        swapped,
                        acts,
                        grads_all,
                        parts,
                        gots,
                        received,
                        partials,
                    )
                )
            )
            if step >= 1:
                done = step if step < mv.planes else 0
                total = parts.pop(done) + gots.pop(done).astype(F32)
                if received is not None:
                    total = total + received.astype(F32)
                    received = None
                if done:
                    sends[done] = total.astype(BF)
        grad_norm_two = total
        attended_both, norm_both = swapped
        branch_mine, branch_got, down_partial = partials

        def branch_step(ring, received):
            at_piece = order[ring]
            branch = branch_mine[at_piece].astype(F32) + branch_got[at_piece].astype(F32)
            return branch if received is None else branch + received.astype(F32)

        def ffn_sum(value):
            return lax.psum_scatter(
                value, "dp", scatter_dimension=0, tiled=True, axis_index_groups=mv.squares()
            )

        down_sum = ffn_sum(down_partial)
        branch_sent = branch_step(0, None).astype(BF)
        grad_norm_two, branch_sent = fence((grad_norm_two, branch_sent))
        branch_ring = mv.up(branch_sent)

        _, norm_two_back = jax.vjp(rms_scale, hidden_one, gain_two)
        grad_rms_two, grad_gain_two = norm_two_back(grad_norm_two)
        grad_hidden = cotangent.astype(F32) + grad_rms_two
        grad_hidden_b = grad_hidden.astype(BF)

        out_partial = dot_tn(attended_both, core_half(mv, grad_hidden_b), BF)
        grad_attended = dot_nt(grad_hidden_b, w_out).astype(BF)
        out_partial, grad_attended, grads_all, norm_all, branch_ring = fence(
            (out_partial, grad_attended, grads_all, norm_all, branch_ring)
        )
        held = {"attended": grad_attended, "grads": grads_all, "norm": norm_all, "out": out_partial, "branch": branch_ring}

        def scores_back(grad_attended):
            grad_probs = jnp.einsum(
                "sqhd,skd->shqk", grad_attended, value, preferred_element_type=F32
            )
            return (
                soft * (grad_probs - jnp.sum(grad_probs * soft, axis=-1, keepdims=True))
            ).astype(BF)

        def lin_back(grad_scores, grad_attended):
            grad_value = jnp.einsum(
                "shqk,sqhd->skd", probs, grad_attended, preferred_element_type=F32
            ).reshape(rows, HD)
            grad_query = jnp.einsum(
                "shqk,skd->sqhd", grad_scores, key, preferred_element_type=F32
            ).reshape(rows, H, HD)
            grad_key = jnp.einsum(
                "shqk,sqhd->skd", grad_scores, query, preferred_element_type=F32
            ).reshape(rows, HD)
            grad_kv_lin = jnp.concatenate(
                [rotate(grad_key, cosine, -sine), grad_value], 1
            ).astype(BF)
            grad_q_lin = (
                rotate(grad_query * head_scale, cosine[:, None, :], -sine[:, None, :])
                .reshape(rows, H * HD)
                .astype(BF)
            )
            return grad_q_lin, grad_kv_lin

        chip = D // (n // 2)
        plane = 4 * chip

        class Scatter:
            def __init__(self, base, chip):
                self.base, self.chip, self.half, self.at = base, chip, chip // 2, 0

            def block(self, array, flip_y, flip_x, low=True, high=True):
                index = (mv.y ^ flip_y) * 2 + (mv.x ^ flip_x)
                start = self.base + index * self.chip + (0 if low else self.half)
                count = self.half * (low + high)
                return lax.dynamic_slice(array, (start, 0), (count, array.shape[1]))

            def open(self, array, send_x, send_y):
                send_x += [
                    self.block(array, 1, 1, high=False),
                    self.block(array, 0, 1, high=False),
                ]
                send_y += [
                    self.block(array, 1, 1, low=False),
                    self.block(array, 1, 0, low=False),
                ]

            def close(self, array, got, send_x, send_y):
                from_x, from_y = got
                self.at = sum(v.shape[0] for v in send_x)
                last_x = self.block(array, 0, 1, low=False).astype(F32)
                last_y = self.block(array, 1, 0, high=False).astype(F32)
                send_x.append((last_x + from_y[: self.half].astype(F32)).astype(BF))
                send_y.append((last_y + from_x[: self.half].astype(F32)).astype(BF))

            def total(self, array, got, more):
                (from_x, from_y), (more_x, more_y) = got, more
                last = slice(self.at, self.at + self.half)
                kept = slice(self.half, self.chip)
                sums = self.block(array, 0, 0).astype(F32)
                sums += jnp.concatenate([from_x[kept], more_x[last]], 0).astype(F32)
                sums += jnp.concatenate([more_y[last], from_y[kept]], 0).astype(F32)
                return sums

        def exchange(send_x, send_y):
            if not send_x:
                return None
            send_x, send_y, now = fence(
                (jnp.concatenate(send_x, 0), jnp.concatenate(send_y, 0), held)
            )
            held.update(now)
            return mv.over_x(send_x), mv.over_y(send_y)

        planes = mv.planes
        lin_items = [Scatter(((mv.z - k) % planes) * plane, chip) for k in [*range(1, planes), 0]]
        out_item = Scatter(0, chip)
        ffn_items = [Scatter(0, padded), Scatter(0, padded)]
        open_lin, open_out = 2, max(4, planes)
        last_round = max(open_lin + planes + 1, open_out + 2, 6 + (planes - 2) // 3, 2 * planes - 3)
        for at in range(last_round + 1):
            now = fence(held)
            held.update(now)
            send_x, send_y = [], []
            j = at - open_lin
            if 0 <= j < planes:
                lin_items[j].open(held["lin"], send_x, send_y)
            if 0 <= j - 1 < planes:
                lin_items[j - 1].close(held["lin"], held["lin1"], send_x, send_y)
            out_x, out_y = [], []
            if at == open_out:
                out_item.open(held["out_b"], out_x, out_y)
            if at == open_out + 1:
                out_item.close(held["out_b"], held["out1"], out_x, out_y)
            ffn_x, ffn_y = [], []
            f = at - 1
            if 0 <= f < 2:
                ffn_items[f].open(held["partials"][f], ffn_x, ffn_y)
            if 0 <= f - 1 < 2:
                ffn_items[f - 1].close(held["partials"][f - 1], held["ffn1"], ffn_x, ffn_y)
            got, got_out = exchange(send_x, send_y), exchange(out_x, out_y)
            got_ffn = exchange(ffn_x, ffn_y)
            if at < planes - 1:
                z = (mv.z - at - 1) % planes
                rows_out = lax.dynamic_slice(held["out"], (z * plane, 0), (plane, D // 2))
                if at > 0:
                    rows_out = rows_out.astype(F32) + held.pop("out_ring").astype(F32)
                held["out_ring"] = mv.up(rows_out.astype(BF))
            if at == planes - 1:
                rows_out = lax.dynamic_slice(held.pop("out"), (mv.z * plane, 0), (plane, D // 2))
                rows_out = rows_out.astype(F32) + held.pop("out_ring").astype(F32)
                held["out_b"] = rows_out.astype(BF)
            ring = at - (planes - 1) + 1
            if 1 <= ring < planes:
                branch = branch_step(ring, held.pop("branch"))
                if ring < planes - 1:
                    held["branch"] = mv.up(branch.astype(BF))
                else:
                    held["output"] = (hidden_one + branch + bias_down).astype(BF)
            if 0 <= j - 2 < planes:
                sums = lin_items[j - 2].total(held["lin"], held["lin2"], held["lin1"])
                if j - 2 > 0:
                    sums = sums + held.pop("lin_ring").astype(F32)
                if j - 2 < planes - 1:
                    held["lin_ring"] = mv.up(sums.astype(BF))
                else:
                    held["lin_sum"] = sums
            if at == open_out + 2:
                sums = out_item.total(held["out_b"], held["out2"], held["out1"])
                held["out_grad"] = jnp.concatenate(swap_halves(mv, sums), 1)
            if 0 <= f - 2 < 2:
                sums = ffn_items[f - 2].total(
                    held["partials"][f - 2], held["ffn2"], held["ffn1"]
                )
                held[f"unit_grad{f - 2}"] = sums[:units]
            for one, two, new in (("ffn1", "ffn2", got_ffn),):
                if one in held:
                    held[two] = held.pop(one)
                if new is not None:
                    held[one] = new
            if "lin1" in held:
                held["lin2"] = held.pop("lin1")
            if got is not None:
                held["lin1"] = got
            if "out1" in held:
                held["out2"] = held.pop("out1")
            if got_out is not None:
                held["out1"] = got_out
            if at == 0:
                held["down_sum"] = down_sum
                held["attended"] = held["attended"].reshape(seqs, LENGTH, H, HD)
                held["scores"] = scores_back(held["attended"])
                partials = [dot_tn(v, held["norm"], BF) for v in held["grads"]]
                held["partials"] = partials
            if at == 1:
                held["q"], held["kv"] = lin_back(held.pop("scores"), held.pop("attended"))
            if at == 1:
                both = jnp.concatenate([core_half(mv, held["q"]), core_half(mv, held["kv"])], 1)
                held["lin"] = dot_tn(norm_both, both, BF)
            if at == 2:
                grad_norm_one = dot_nt(held.pop("q"), w_query) + dot_nt(held.pop("kv"), w_keyval)
                _, norm_one_back = jax.vjp(rms_scale, x_value, gain_one)
                grad_rms_one, grad_gain_one = norm_one_back(grad_norm_one)
                held["input_grad"] = (grad_hidden + grad_rms_one).astype(BF)
                down_bias_sum = jnp.sum(cotangent, axis=0, dtype=F32)
                part = D // n
                small = jnp.stack([grad_gain_one, grad_gain_two, down_bias_sum])
                small = small.reshape(3, planes, 2, 2, 2, part).transpose(2, 3, 4, 1, 0, 5)
                held["small"] = small
                bias = jnp.stack([jnp.sum(v, axis=0, dtype=F32) for v in held.pop("grads")])
                bias = bias.reshape(2, 2, 2, padded)[..., :units]
                held["bias"] = bias.transpose(1, 2, 0, 3)
            for stage, (coordinate, move) in enumerate(
                ((mv.y, mv.over_y), (mv.x, mv.over_x), (mv.core, mv.other))
            ):
                if at == 3 + stage:
                    for name in ("small", "bias")[: 2 if stage < 2 else 1]:
                        whole = held[name]
                        keep = lax.dynamic_index_in_dim(whole, coordinate, 0, keepdims=False)
                        away = lax.dynamic_index_in_dim(whole, 1 - coordinate, 0, keepdims=False)
                        held[name] = keep + move(away)
            for step in range(1, planes):
                if at == min(6 + (step - 1) // 3, last_round):
                    away = lax.dynamic_index_in_dim(
                        held["small"], (mv.z + step) % planes, 0, keepdims=False
                    )
                    held["small_sum"] = held.get("small_sum", 0.0) + mv.up(away, step)
            if at == last_round - 1:
                held["down_grad"] = held.pop("down_sum")[:units].astype(F32)

        small = held["small_sum"] + lax.dynamic_index_in_dim(
            held["small"], mv.z, 0, keepdims=False
        )
        down_grad, gate_grad, up_grad = (
            held[k] for k in ("down_grad", "unit_grad0", "unit_grad1")
        )
        first, second = swap_halves(mv, held["lin_sum"])
        q_grad = jnp.concatenate([first[:, : D // 2], second[:, : D // 2]], 1)
        kv_grad = jnp.concatenate([first[:, D // 2 :], second[:, D // 2 :]], 1)

        return (
            held["output"],
            held["input_grad"],
            small[0],
            q_grad,
            kv_grad,
            held["out_grad"],
            small[1],
            gate_grad,
            held["bias"][0],
            up_grad,
            held["bias"][1],
            down_grad,
            small[2],
        )

    return body


def solution(mesh):
    matrix, vector = P("dp", None), P("dp")
    return jax.shard_map(
        make_body(mesh.shape["dp"]),
        mesh=mesh,
        in_specs=(
            matrix,
            vector,
            vector,
            matrix,
            matrix,
            matrix,
            vector,
            matrix,
            vector,
            matrix,
            vector,
            matrix,
            vector,
            matrix,
        ),
        out_specs=(
            matrix,
            matrix,
            vector,
            matrix,
            matrix,
            matrix,
            vector,
            matrix,
            vector,
            matrix,
            vector,
            matrix,
            vector,
        ),
        check_vma=False,
    )
```
